256 devices in a mesh: row: 32 (over x_lo, z, core), col: 8 (over x_hi, y).
Axes of the slice: x: 4 (x_hi: 2, x_lo: 2; x = x_hi * 2 + x_lo), y: 4, z: 8, core: 2. Of those that a mesh axis runs over, the one named last changes fastest.
Arguments:
- amplitudes: float32 [4096, 8192], P(('col', 'row')), may hold values from -6 to 6
- integrals: float32 [8192, 8192], P('col', 'row'), may hold values from -0.0625 to 0.0625
- other_terms: float32 [4096, 8192], P('col', 'row'), may hold values from -6 to 6
- occupied_first: int32 [4096], P('col'), may hold values from 0 to 99
- occupied_second: int32 [4096], P('col'), may hold values from 0 to 99
- virtual_first: int32 [8192], P('row'), may hold values from 0 to 599
- virtual_second: int32 [8192], P('row'), may hold values from 0 to 599
- occupied_energy: float32 [100], replicated, may hold values from -2 to -0.5
- virtual_energy: float32 [600], replicated, may hold values from 0.2 to 2.5
Outputs:
- new_amplitudes: float32 [4096, 8192], P('col', 'row')
The draws below stay inside these ranges and needn't reach their ends.
All inputs are finite; a program needn't handle non-finite values.
Results may differ from the reference program's by a relative error of at most 0.000068.
Values sent between devices are 32-bit elements; how exact they have to be, the bound alone decides.
A program may use at most 128 MiB of HBM per device.

```python
import jax
import jax.numpy as jnp
from jax import lax

NOCC = 100
NVIR = 600
VP = 8192
OP = 4096


def with_ends(result, rng, least, largest):
    place = [jax.random.randint(jax.random.fold_in(rng, axis), (), 0, length) for axis, length in enumerate(result.shape)]
    widest = result.shape.index(max(result.shape))
    beside = place[:widest] + [(place[widest] + 1) % result.shape[widest]] + place[widest + 1:]
    return result.at[tuple(place)].set(least).at[tuple(beside)].set(largest)


def shard_levels(rng, extent, pieces, least, top_value):
    loudness, own = 1.0, jax.random.fold_in(rng, 6)
    for dim, parts in pieces:
        steps = jnp.exp(jax.random.uniform(jax.random.fold_in(own, dim), (parts,), jnp.float32, least / len(pieces), top_value / len(pieces)))
        loudness = loudness * jnp.repeat(steps, extent[dim] // parts).reshape([-1 if axis == dim else 1 for axis in range(len(extent))])
    return loudness


def gaussian(key, extent, spread, limit, cuts=(), kind=jnp.bfloat16):
    values = spread * jax.random.normal(key, extent, jnp.float32)
    if cuts:
        values = values * shard_levels(key, extent, cuts, -0.22, 0.18)
    return jnp.clip(values, -limit, limit).astype(kind)


def setup_inputs(seed: int = 0) -> dict:
    key_of = jax.random.split(jax.random.key(seed), 10)
    amplitudes = gaussian(key_of[0], (OP, VP), 1.0, 6.0, ((0, 256),), jnp.float32)
    integrals = gaussian(key_of[1], (VP, VP), VP ** -0.5, 0.0625, ((0, 8), (1, 32)), jnp.float32)
    other_terms = gaussian(key_of[2], (OP, VP), 1.0, 6.0, ((0, 8), (1, 32)), jnp.float32)
    occupied_first = with_ends(jax.random.randint(key_of[3], (OP,), 0, NOCC), jax.random.fold_in(key_of[3], 1), 0, NOCC - 1).astype(jnp.int32)
    occupied_second = with_ends(jax.random.randint(key_of[4], (OP,), 0, NOCC), jax.random.fold_in(key_of[4], 1), 0, NOCC - 1).astype(jnp.int32)
    virtual_first = with_ends(jax.random.randint(key_of[5], (VP,), 0, NVIR), jax.random.fold_in(key_of[5], 1), 0, NVIR - 1).astype(jnp.int32)
    virtual_second = with_ends(jax.random.randint(key_of[6], (VP,), 0, NVIR), jax.random.fold_in(key_of[6], 1), 0, NVIR - 1).astype(jnp.int32)
    occupied_energy = jnp.clip(jax.random.uniform(key_of[7], (NOCC,), jnp.float32, -2.0, -0.5), -2.0, -0.5)
    virtual_energy = jnp.clip(jax.random.uniform(key_of[8], (NVIR,), jnp.float32, 0.2, 2.5), 0.2, 2.5)
    return {"amplitudes": amplitudes, "integrals": integrals, "other_terms": other_terms, "occupied_first": occupied_first, "occupied_second": occupied_second, "virtual_first": virtual_first, "virtual_second": virtual_second, "occupied_energy": occupied_energy, "virtual_energy": virtual_energy}


def reference(amplitudes, integrals, other_terms, occupied_first, occupied_second, virtual_first, virtual_second, occupied_energy, virtual_energy):
    occupied_sum = occupied_energy[occupied_first] + occupied_energy[occupied_second]
    virtual_sum = virtual_energy[virtual_first] + virtual_energy[virtual_second]
    denominator = virtual_sum[None, :] - occupied_sum[:, None]
    ladder = jnp.dot(amplitudes, integrals, precision=lax.Precision.HIGHEST, preferred_element_type=jnp.float32)
    return amplitudes + (other_terms + ladder) / denominator
```

```python
import functools

import jax
import jax.numpy as jnp
from jax import lax
from jax.experimental import pallas as pl
from jax.experimental.pallas import tpu as pltpu
from jax.sharding import PartitionSpec as P

MESH = pl.DeviceIdType.MESH
F32, BF16 = jnp.float32, jnp.bfloat16
BASE = (0, 128, 384, 640, 896)
SIZE = (128, 256, 256, 256, 128)


def lookup(index_ref, table_ref):
    n = table_ref.shape[1]
    onehot = (lax.broadcasted_iota(jnp.int32, (n, index_ref.shape[1]), 0) == index_ref[...]).astype(F32)
    table = jnp.broadcast_to(table_ref[...], (8, n))
    return jnp.dot(table, onehot, precision=lax.Precision.HIGHEST, preferred_element_type=F32)


def kernel(
    a_ref, b_ref, other_ref, of_ref, os_ref, vf_ref, vs_ref, oe_ref, ve_ref,
    out_ref,
    abuf, ahi, alo, bbuf, bhi, blo, cbuf, rbuf, occ_row, occ_col, vsum,
    loc_sem, zs, zr, xs, xr, ss, sr, ys, yr, es, er, cs, cr, ts, tr,
):
    row, col = lax.axis_index("row"), lax.axis_index("col")
    xl, z, c = row // 16, (row // 2) % 8, row % 2
    xh, y = col // 4, col % 4

    def dev(xh, xl, y, z, c):
        return (xl * 16 + z * 2 + c, xh * 4 + y)

    px = ((xh, xl), (xh, 1 - xl), (1 - xh, 1 - xl), (1 - xh, xl))
    xdev = [dev(h, l, y, z, c) for h, l in px]
    zp, zm = (z + 1) % 8, (z + 7) % 8
    yp, ym = (y + 1) % 4, (y + 3) % 4
    zdev = (dev(xh, xl, y, zp, c), dev(xh, xl, y, zm, c))
    ydev = (dev(xh, xl, yp, z, c), dev(xh, xl, ym, z, c))
    sib = dev(xh, xl, y, z, 1 - c)

    def zof(s, p):
        return (z + 8 - s) % 8 if p == 0 else (z + s) % 8

    xi = [h * 2 + l for h, l in px]

    def remote(src, dst, send, recv, to):
        return pltpu.make_async_remote_copy(
            src_ref=src, dst_ref=dst, send_sem=send, recv_sem=recv, device_id=to, device_id_type=MESH
        )

    own_a = pltpu.make_async_copy(a_ref.at[:, xh, :, xl], abuf.at[z, xi[0], c], loc_sem.at[0])
    own_b = pltpu.make_async_copy(b_ref.at[:, xl], bbuf.at[0, y], loc_sem.at[1])
    own_o = pltpu.make_async_copy(other_ref, out_ref, loc_sem.at[2])
    own_a.start()
    own_b.start()
    own_o.start()

    barrier = pltpu.get_barrier_semaphore()
    for to in (*xdev[1:], *zdev, *ydev, sib):
        pl.semaphore_signal(barrier, inc=1, device_id=to, device_id_type=MESH)
    occ_row[0] = lookup(of_ref, oe_ref) + lookup(os_ref, oe_ref)
    vsum[0] = lookup(vf_ref, ve_ref) + lookup(vs_ref, ve_ref)
    pl.semaphore_wait(barrier, 8)

    sent = []

    def go(copy):
        copy.start()
        sent.append(copy)

    def z_send(s, q, d):
        where = (zof(s, d), xi[q], c)
        src = a_ref.at[:, xh, :, xl] if s == 0 and q == 0 else abuf.at[where]
        go(remote(src, abuf.at[where], zs.at[d, s, q], zr.at[d, s, q], zdev[d]))

    def z_wait(s, q, d):
        where = (zof(s, d), xi[q], c)
        remote(abuf.at[where], abuf.at[where], zs.at[d, s - 1, q], zr.at[d, s - 1, q], zdev[d]).wait_recv()

    def sib_copy(s, p, core):
        where = abuf.at[zof(s, p), :, core]
        i = 0 if s == 0 else 2 * s - 1 + p
        return remote(where, where, ss.at[i], sr.at[i], sib)

    for d in range(2):
        z_send(0, 0, d)
    for q in (1, 2, 3):
        go(
            remote(
                a_ref.at[:, px[q][0], :, px[q][1]], abuf.at[z, xi[0], c], xs.at[q - 1], xr.at[q - 1], xdev[q]
            )
        )
    for d in range(2):
        go(remote(b_ref.at[:, xl], bbuf.at[0, y], ys.at[0, d], yr.at[0, d], ydev[d]))
    go(remote(occ_row.at[0], occ_row.at[1], ts.at[0], tr.at[0], xdev[3]))
    go(remote(vsum.at[0], vsum.at[1], ts.at[1], tr.at[1], xdev[1]))
    own_a.wait()

    for q in (1, 2, 3):
        remote(abuf.at[z, xi[q], c], abuf.at[z, xi[q], c], xs.at[q - 1], xr.at[q - 1], xdev[q]).wait_recv()
        for d in range(2):
            z_send(0, q, d)
    go(sib_copy(0, 0, c))
    go(remote(b_ref.at[:, 1 - xl], bbuf.at[1, y], es.at[0], er.at[0], xdev[1]))

    def split_b(h, yy, g0, n):
        @pl.loop(0, n * 4)
        def _(i):
            g, r = g0 + i // 4, (i % 4) * 32
            r = pl.multiple_of(r, 32)
            v = bbuf[h, yy, g, pl.ds(r, 32), :]
            hi = v.astype(BF16)
            to = pl.ds(pl.multiple_of(yy * 512 + g * 128 + r, 32), 32)
            bhi[h, to, :] = hi
            blo[h, to, :] = (v - hi.astype(F32)).astype(BF16)

    def split_a(s):
        n = 1 if s in (0, 4) else 2

        @pl.loop(0, 16)
        def _(j):
            lanes = pl.ds(pl.multiple_of(j * 128, 128), 128)
            for p in range(n):
                for h in range(2):
                    v = abuf[zof(s, p), 2 * h : 2 * h + 2, :, :, j].reshape(64, 128)
                    hi = v.astype(BF16)
                    r = BASE[s] + h * (SIZE[s] // 2) + p * 64
                    ahi[r : r + 64, lanes] = hi
                    alo[r : r + 64, lanes] = (v - hi.astype(F32)).astype(BF16)

    mine = z * 2 + c
    half = pl.ds(pl.multiple_of(xl * 128, 128), 128)
    panel_h = jnp.where(xh == xl, 0, 1)

    def unit(s, h):
        r0, n = BASE[s], SIZE[s]
        rows = slice(r0, r0 + n)
        cbuf[h, rows, :] = (
            jnp.dot(alo[rows, :], bhi[h], preferred_element_type=F32)
            + jnp.dot(ahi[rows, :], blo[h], preferred_element_type=F32)
            + jnp.dot(ahi[rows, :], bhi[h], preferred_element_type=F32)
        )

        @pl.when(panel_h == h)
        def _():
            for p in range(n // 128):
                zz = zof(s, p)
                for k in range(2):
                    v = abuf[zz, 2 * k : 2 * k + 2, :, :, mine].reshape(64, 128)
                    for l in range(2):
                        o = occ_col[jnp.where(xh == k, 0, 1), pl.ds(pl.multiple_of(l * 256 + zz * 32, 32), 32), :]
                        d = vsum[h, 0:1, half] - o
                        r = r0 + k * (n // 2) + p * 64 + l * 32
                        cbuf[h, r : r + 32, half] += v[l * 32 : l * 32 + 32] * d

        def part(k):
            return cbuf.at[h, pl.ds(pl.multiple_of(r0 + k * (n // 2), 64), n // 2)]

        def to(q):
            return rbuf.at[q - 1, pl.ds(r0 // 2, n // 2)]

        if h == 0:
            go(remote(part(1 - xh), to(3), cs.at[s, 2], cr.at[s, 2], xdev[3]))
        else:
            go(remote(part(xh), to(1), cs.at[s, 0], cr.at[s, 0], xdev[1]))
            go(remote(part(1 - xh), to(2), cs.at[s, 1], cr.at[s, 1], xdev[2]))

    def finish(s):
        r0, n = BASE[s], SIZE[s]
        for q in (1, 2, 3):
            at = rbuf.at[q - 1, pl.ds(r0 // 2, n // 2)]
            remote(at, at, cs.at[s, q - 1], cr.at[s, q - 1], xdev[q]).wait_recv()
        for p in range(n // 128):
            zz = zof(s, p)
            for l in range(2):
                r = p * 64 + l * 32
                here = pl.ds(pl.multiple_of(r0 + xh * (n // 2) + r, 32), 32)
                there = pl.ds(r0 // 2 + r, 32)
                at = pl.ds(pl.multiple_of(l * 256 + zz * 32, 32), 32)
                total = cbuf[0, here, :] + rbuf[0, there, :] + rbuf[1, there, :] + rbuf[2, there, :]
                o = occ_col[0, at, :]
                d = vsum[0, 0:1, :] - jnp.concatenate([o, o], axis=1)
                out_ref[at, :] = (out_ref[at, :] + total) / d

    def y_wait(h, i):
        if i < 2:
            at = bbuf.at[h, (ym, yp)[i]]
        else:
            at = bbuf.at[h, (y + 2) % 4, pl.ds(2 * (i - 2), 2)]
        remote(at, at, ys.at[h, i], yr.at[h, i], ydev[i % 2]).wait_recv()

    def y_forward(h):
        for d in range(2):
            at = bbuf.at[h, (ym, yp)[d], pl.ds(2 * d, 2)]
            go(remote(at, at, ys.at[h, 2 + d], yr.at[h, 2 + d], ydev[d]))

    def z_step(s, qs):
        for q in qs:
            for d in range(2):
                if s == 4 and d != q // 2:
                    continue
                z_wait(s, q, d)
                if s < 3 or (s == 3 and d == q // 2):
                    z_send(s, q, d)

    def sib_send(s):
        for p in range(1 if s in (0, 4) else 2):
            go(sib_copy(s, p, c))

    def sib_wait(s):
        for p in range(1 if s in (0, 4) else 2):
            sib_copy(s, p, 1 - c).wait_recv()

    for k, at in ((0, occ_row.at[0]), (1, occ_row.at[1])):
        if k == 1:
            remote(at, at, ts.at[0], tr.at[0], xdev[3]).wait_recv()
        occ_col[k] = jnp.broadcast_to(at[0:1, :], (128, 512)).T
    remote(vsum.at[1], vsum.at[1], ts.at[1], tr.at[1], xdev[1]).wait_recv()
    own_b.wait()
    split_b(0, y, 0, 4)
    z_step(1, (0, 1))
    sib_wait(0)
    split_a(0)
    z_step(1, (2, 3))
    sib_send(1)
    y_wait(0, 0)
    y_wait(0, 1)
    y_forward(0)
    split_b(0, ym, 0, 4)
    split_b(0, yp, 0, 4)
    remote(bbuf.at[1, y], bbuf.at[1, y], es.at[0], er.at[0], xdev[1]).wait_recv()
    for d in range(2):
        go(remote(bbuf.at[1, y], bbuf.at[1, y], ys.at[1, d], yr.at[1, d], ydev[d]))
    sib_wait(1)
    split_a(1)
    split_b(1, y, 0, 4)
    z_step(2, (0, 1))
    y_wait(0, 2)
    y_wait(0, 3)
    split_b(0, (y + 2) % 4, 0, 4)
    unit(0, 0)
    unit(1, 0)
    z_step(2, (2, 3))
    sib_send(2)
    z_step(3, (0,))
    sib_wait(2)
    split_a(2)
    unit(2, 0)
    y_wait(1, 0)
    y_wait(1, 1)
    y_forward(1)
    z_step(3, (1,))
    split_b(1, ym, 0, 4)
    split_b(1, yp, 0, 4)
    z_step(3, (2, 3))
    sib_send(3)
    y_wait(1, 2)
    y_wait(1, 3)
    split_b(1, (y + 2) % 4, 0, 4)
    unit(0, 1)
    unit(1, 1)
    unit(2, 1)
    sib_wait(3)
    split_a(3)
    unit(3, 1)
    unit(3, 0)
    z_step(4, (0, 2, 1, 3))
    sib_send(4)
    own_o.wait()
    finish(0)
    sib_wait(4)
    split_a(4)
    unit(4, 1)
    unit(4, 0)
    for s in (1, 2, 3, 4):
        finish(s)
    for copy in sent:
        copy.wait_send()


def local(amplitudes, integrals, other_terms, of, os_, vf, vs, oe, ve):
    a = amplitudes.reshape(2, 8, 64, 128).transpose(0, 2, 1, 3).reshape(2, 2, 16, 2, 8, 128)
    b = integrals.reshape(4, 2, 128, 256)
    any_, vmem = pl.BlockSpec(memory_space=pl.ANY), pl.BlockSpec(memory_space=pltpu.VMEM)
    dma = pltpu.SemaphoreType.DMA
    return pl.pallas_call(
        kernel,
        out_shape=jax.ShapeDtypeStruct((512, 256), F32),
        in_specs=[any_, any_, any_] + [vmem] * 6,
        out_specs=vmem,
        scratch_shapes=[
            pltpu.VMEM((8, 4, 2, 2, 16, 8, 128), F32),
            pltpu.VMEM((1024, 2048), BF16),
            pltpu.VMEM((1024, 2048), BF16),
            pltpu.VMEM((2, 4, 4, 128, 256), F32),
            pltpu.VMEM((2, 2048, 256), BF16),
            pltpu.VMEM((2, 2048, 256), BF16),
            pltpu.VMEM((2, 1024, 256), F32),
            pltpu.VMEM((3, 512, 256), F32),
            pltpu.VMEM((2, 8, 512), F32),
            pltpu.VMEM((2, 512, 128), F32),
            pltpu.VMEM((2, 8, 256), F32),
            dma((3,)),
            dma((2, 4, 4)), dma((2, 4, 4)),
            dma((3,)), dma((3,)),
            dma((8,)), dma((8,)),
            dma((2, 4)), dma((2, 4)),
            dma((1,)), dma((1,)),
            dma((5, 3)), dma((5, 3)),
            dma((2,)), dma((2,)),
        ],
        compiler_params=pltpu.CompilerParams(
            collective_id=0, has_side_effects=True, vmem_limit_bytes=48 << 20
        ),
        cost_estimate=pl.CostEstimate(flops=6442450944, bytes_accessed=4 << 20, transcendentals=0),
    )(
        a, b, other_terms,
        of.reshape(1, -1), os_.reshape(1, -1), vf.reshape(1, -1), vs.reshape(1, -1),
        oe.reshape(1, -1), ve.reshape(1, -1),
    )


def solution(mesh):
    in_specs = (
        P(("col", "row"), None),
        P("col", "row"),
        P("col", "row"),
        P("col"),
        P("col"),
        P("row"),
        P("row"),
        P(),
        P(),
    )
    return jax.shard_map(local, mesh=mesh, in_specs=in_specs, out_specs=P("col", "row"), check_vma=False)
```

```python
import jax
import jax.numpy as jnp
from jax import lax
from jax.experimental import pallas as pl
from jax.experimental.pallas import tpu as pltpu
from jax.sharding import PartitionSpec as P

MESH = pl.DeviceIdType.MESH
F32, BF16 = jnp.float32, jnp.bfloat16
START = (0, 64, 192, 320, 448, 512)
ORDER = (
    (0, 0), (1, 0), (2, 0), (5, 0), (3, 0), (4, 0),
    (1, 1), (2, 1), (3, 1), (4, 1), (0, 1), (5, 1), (6, 1), (6, 0), (7, 1), (7, 0),
)


def lookup(index_ref, table_ref):
    n = table_ref.shape[-1]
    onehot = (lax.broadcasted_iota(jnp.int32, (n, index_ref.shape[1]), 0) == index_ref[...]).astype(F32)
    table = jnp.broadcast_to(table_ref[...].reshape(1, n), (8, n))
    return jnp.dot(table, onehot, precision=lax.Precision.HIGHEST, preferred_element_type=F32)


def kernel(
    a_ref, b_ref, other_ref, *refs
):
    small, out_ref, refs = refs[:6], refs[6], refs[7:]
    abuf, ahi, alo, bbuf, bhi, blo, cbuf, rbuf, occ_row, occ_col, vsum, obuf = refs[:12]
    small_v, (loc, zr, xr, sr, yr, er, cr, tr, os, sends) = refs[12:18], refs[18:]
    of_ref, os_ref, vf_ref, vs_ref, oe_ref, ve_ref = small_v
    row, col = lax.axis_index("row"), lax.axis_index("col")
    xl, z, c = row // 16, (row // 2) % 8, row % 2
    xh, y = col // 4, col % 4

    def dev(xh, xl, y, z, c):
        return (xl * 16 + z * 2 + c, xh * 4 + y)

    px = ((xh, xl), (xh, 1 - xl), (1 - xh, 1 - xl), (1 - xh, xl))
    xi = [h * 2 + l for h, l in px]
    xdev = [dev(h, l, y, z, c) for h, l in px]
    zp, zm = (z + 1) % 8, (z + 7) % 8
    yp, ym, y2 = (y + 1) % 4, (y + 3) % 4, (y + 2) % 4
    zdev = (dev(xh, xl, y, zp, c), dev(xh, xl, y, zm, c))
    ydev = (dev(xh, xl, yp, z, c), dev(xh, xl, ym, z, c))
    sib = dev(xh, xl, y, z, 1 - c)

    def sides(s):
        return range(1 if s in (0, 4) else 2)

    zs_of = [((z + 8 - s) % 8, (z + s) % 8) for s in range(5)]

    def zof(s, p):
        return zs_of[s][p]

    def remote(src, dst, recv, to):
        return pltpu.make_async_remote_copy(
            src_ref=src, dst_ref=dst, send_sem=sends, recv_sem=recv, device_id=to, device_id_type=MESH
        )

    sent = []

    def go(make):
        make().start()
        sent.append(make)

    barrier = pltpu.get_barrier_semaphore()
    for to in (*xdev[1:], *zdev, *ydev, sib):
        pl.semaphore_signal(barrier, inc=1, device_id=to, device_id_type=MESH)
    local = [pltpu.make_async_copy(src, dst, loc.at[i]) for i, (src, dst) in enumerate(zip(small, small_v))]
    own_a = pltpu.make_async_copy(a_ref.at[:, xh, :, xl], abuf.at[z, xi[0], c], loc.at[6])
    own_b = pltpu.make_async_copy(b_ref.at[:, xl], bbuf.at[0, y], loc.at[7])
    own_o = pltpu.make_async_copy(other_ref, obuf, loc.at[8])
    for copy in (own_a, *local, own_b, own_o):
        copy.start()

    def arrive(at, recv):
        remote(at, at, recv, sib).wait_recv()

    def z_sem(s, q, d):
        return zr.at[(s - 1) * 8 + d * 4 + q if s < 4 else 24 + q]

    def z_send(s, q, d):
        def make():
            where = abuf.at[zof(s, d), xi[q], c]
            src = a_ref.at[:, xh, :, xl] if s == 0 and q == 0 else where
            return remote(src, where, z_sem(s + 1, q, d), zdev[d])

        go(make)

    def z_step(s, q):
        for d in range(2):
            if s == 4 and d != q // 2:
                continue
            arrive(abuf.at[zof(s, d), xi[q], c], z_sem(s, q, d))
            if s < 3 or (s == 3 and d == q // 2):
                z_send(s, q, d)

    def x_send(q):
        go(lambda: remote(a_ref.at[:, px[q][0], :, px[q][1]], abuf.at[z, xi[0], c], xr.at[q - 1], xdev[q]))

    def x_step(q):
        arrive(abuf.at[z, xi[q], c], xr.at[q - 1])
        for d in range(2):
            z_send(0, q, d)

    def sib_at(s, p, k, core):
        if s == 4:
            return abuf.at[zof(s, 0), xi[k], core], sr.at[14 + k]
        where = abuf.at[zof(s, p), pl.ds(2 * (xh if k == 0 else 1 - xh), 2), core]
        return where, sr.at[2 * (0 if s == 0 else 2 * s - 1 + p) + k]

    def sib_send(s, k):
        for p in sides(s):

            def make(p=p):
                where, sem = sib_at(s, p, k, c)
                return remote(where, where, sem, sib)

            go(make)

    def sib_wait(s, k):
        for p in sides(s):
            arrive(*sib_at(s, p, k, 1 - c))

    def part(i, d):
        return pl.ds(2 * (i if d == 0 else 1 - i), 2)

    def y_send(h):
        for i in range(2):
            for d in range(2):

                def make(i=i, d=d):
                    src = b_ref.at[part(i, d), xl] if h == 0 else bbuf.at[h, y, part(i, d)]
                    return remote(src, bbuf.at[h, y, part(i, d)], yr.at[h * 6 + i * 2 + d], ydev[d])

                go(make)

    def y_wait(h, i):
        for d in range(2):
            arrive(bbuf.at[h, (ym, yp)[d], part(i, d)], yr.at[h * 6 + i * 2 + d])

    def y_forward(h):
        for d in range(2):

            def make(d=d):
                at = bbuf.at[h, (ym, yp)[d], part(0, d)]
                return remote(at, at, yr.at[h * 6 + 4 + d], ydev[d])

            go(make)

    def y_far(h):
        for d in range(2):
            arrive(bbuf.at[h, y2, part(0, d)], yr.at[h * 6 + 4 + d])

    def e_send():
        go(lambda: remote(b_ref.at[:, 1 - xl], bbuf.at[1, y], er, xdev[1]))

    def e_wait():
        arrive(bbuf.at[1, y], er)

    def split_b(h, yy):
        @pl.loop(0, 16)
        def _(i):
            g, r = i // 4, pl.multiple_of((i % 4) * 32, 32)
            v = bbuf[h, yy, g, pl.ds(r, 32), :]
            hi = v.astype(BF16)
            to = pl.ds(pl.multiple_of(yy * 512 + g * 128 + r, 32), 32)
            bhi[h, to, :] = hi
            blo[h, to, :] = (v - hi.astype(F32)).astype(BF16)

    def rows_at(s, p, k):
        return (64 * k if s in (0, 4) else 128 * k - 128) + 256 * s - (128 if s == 4 else 0) + 64 * p

    def split_a(s, k):
        @pl.loop(0, 16)
        def _(j):
            lanes = pl.ds(pl.multiple_of(j * 128, 128), 128)
            for p in sides(s):
                v = abuf[zof(s, p), pl.ds(2 * (xh if k == 0 else 1 - xh), 2), :, :, j].reshape(64, 128)
                hi = v.astype(BF16)
                r = rows_at(s, p, k)
                ahi[r : r + 64, lanes] = hi
                alo[r : r + 64, lanes] = (v - hi.astype(F32)).astype(BF16)

    mine = z * 2 + c
    panel_h = jnp.where(xh == xl, 0, 1)

    def block(b, h):
        r0 = pl.multiple_of(b * 128, 128)
        rows = pl.ds(r0, 128)
        cbuf[h, rows, :] = (
            jnp.dot(alo[rows, :], bhi[h], preferred_element_type=F32)
            + jnp.dot(ahi[rows, :], blo[h], preferred_element_type=F32)
            + jnp.dot(ahi[rows, :], bhi[h], preferred_element_type=F32)
        )

        @pl.when(panel_h == h)
        def _():
            lanes = pl.ds(pl.multiple_of(xl * 128, 128), 128)
            s, both = (b + 1) // 2, ((b == 0) | (b == 7)).astype(jnp.int32)
            for g in range(4):
                k = both * (g // 2) + (1 - both) * ((b + 1) % 2)
                up = (1 - both) * (g // 2)
                zz = (z + 8 + (2 * up - 1) * s) % 8
                x = 2 * (xh + k - 2 * xh * k) + g % 2
                v = abuf[zz, x, :, :, mine].reshape(32, 128)
                o = occ_col[k, pl.ds(pl.multiple_of(g % 2 * 256 + zz * 32, 32), 32), :]
                cbuf[h, pl.ds(r0 + 32 * g, 32), lanes] += v * (vsum[h, 0:1, lanes] - o)

    def c_copy(s, k, h):
        q = 3 if h == 0 else 1 + k
        size = START[s + 1] - START[s]
        src = cbuf.at[h, rows_at(s, 0, k) : rows_at(s, 0, k) + size]
        return remote(src, rbuf.at[q - 1, START[s] : START[s] + size], cr.at[s * 3 + q - 1], xdev[q])

    def c_send(s, k, h):
        go(lambda: c_copy(s, k, h))

    def finish(s):
        for k, h in ((1, 0), (0, 1), (1, 1)):
            c_copy(s, k, h).wait_recv()
        for p in sides(s):
            zz = zof(s, p)
            for l in range(2):
                r, t = rows_at(s, p, 0) + l * 32, START[s] + p * 64 + l * 32
                here, there = slice(r, r + 32), slice(t, t + 32)
                at = pl.ds(pl.multiple_of(l * 256 + zz * 32, 32), 32)
                total = (cbuf[0, here, :] + rbuf[2, there, :]) + (rbuf[0, there, :] + rbuf[1, there, :])
                o = occ_col[0, at, :]
                d = vsum[0, 0:1, :] - jnp.concatenate([o, o], axis=1)
                obuf[at, :] = (obuf[at, :] + total) / d
                pltpu.make_async_copy(obuf.at[at], out_ref.at[at], os).start()

    pl.semaphore_wait(barrier, 8)
    for d in range(2):
        z_send(0, 0, d)
    x_send(1)
    x_send(2)
    y_send(0)
    for copy in local:
        copy.wait()
    occ_row[0] = lookup(of_ref, oe_ref) + lookup(os_ref, oe_ref)
    vsum[0] = lookup(vf_ref, ve_ref) + lookup(vs_ref, ve_ref)
    go(lambda: remote(occ_row.at[0], occ_row.at[1], tr.at[0], xdev[3]))
    go(lambda: remote(vsum.at[0], vsum.at[1], tr.at[1], xdev[1]))
    x_step(1)
    x_step(2)
    x_send(3)
    e_send()
    z_step(1, 0)
    own_b.wait()
    split_b(0, y)
    y_wait(0, 0)
    y_forward(0)
    z_step(1, 1)
    x_step(3)
    own_a.wait()
    sib_send(0, 0)
    sib_send(0, 1)
    occ_col[0] = jnp.broadcast_to(occ_row[0, 0:1, :], (128, 512)).T
    arrive(occ_row.at[1], tr.at[0])
    arrive(vsum.at[1], tr.at[1])
    occ_col[1] = jnp.broadcast_to(occ_row[1, 0:1, :], (128, 512)).T
    z_step(1, 2)
    y_wait(0, 1)
    split_b(0, ym)
    split_b(0, yp)
    z_step(2, 0)
    for k in range(2):
        sib_wait(0, k)
        split_a(0, k)
    z_step(2, 1)
    e_wait()
    y_send(1)
    split_b(1, y)
    z_step(1, 3)
    sib_send(1, 0)
    sib_send(1, 1)
    y_far(0)
    split_b(0, y2)

    before = [[] for _ in ORDER]

    def at(j, f, *a):
        before[j].append(lambda: f(*a))

    at(1, c_send, 0, 1, 0)
    at(1, sib_wait, 1, 0)
    at(1, split_a, 1, 0)
    at(1, z_step, 2, 2)
    at(2, sib_wait, 1, 1)
    at(2, split_a, 1, 1)
    at(3, c_send, 1, 1, 0)
    at(3, y_wait, 1, 0)
    at(3, y_forward, 1)
    at(3, z_step, 3, 0)
    at(3, z_step, 3, 1)
    at(3, sib_send, 3, 0)
    at(3, sib_wait, 3, 0)
    at(3, split_a, 3, 0)
    at(4, z_step, 2, 3)
    at(4, sib_send, 2, 0)
    at(4, sib_send, 2, 1)
    at(4, y_wait, 1, 1)
    at(4, split_b, 1, ym)
    at(4, split_b, 1, yp)
    at(4, sib_wait, 2, 0)
    at(4, split_a, 2, 0)
    at(5, sib_wait, 2, 1)
    at(5, split_a, 2, 1)
    at(6, c_send, 2, 1, 0)
    at(6, z_step, 3, 2)
    at(6, y_far, 1)
    at(6, split_b, 1, y2)
    at(7, c_send, 1, 0, 1)
    at(8, c_send, 1, 1, 1)
    for q in (0, 2):
        at(8, z_step, 4, q)
        at(8, sib_send, 4, q)
    at(9, c_send, 2, 0, 1)
    at(10, c_send, 2, 1, 1)
    at(10, z_step, 3, 3)
    at(10, sib_send, 3, 1)
    at(11, c_send, 0, 0, 1)
    at(11, c_send, 0, 1, 1)
    at(12, c_send, 3, 0, 1)
    at(12, sib_wait, 3, 1)
    at(12, split_a, 3, 1)
    at(13, c_send, 3, 1, 1)
    at(14, c_send, 3, 1, 0)
    for q in (1, 3):
        at(14, z_step, 4, q)
        at(14, sib_send, 4, q)
    at(14, own_o.wait)
    for q in (0, 2, 1, 3):
        at(14, sib_wait, 4, q)
    at(14, split_a, 4, 0)
    at(14, split_a, 4, 1)
    at(15, c_send, 4, 0, 1)
    at(15, c_send, 4, 1, 1)

    @pl.loop(0, len(ORDER))
    def _(j):
        for k, steps in enumerate(before):
            if steps:

                @pl.when(j == k)
                def _():
                    for step in steps:
                        step()

        def pick(values):
            result = values[0]
            for i in range(1, len(values)):
                if values[i] != values[i - 1]:
                    result += (values[i] - values[i - 1]) * (j >= i).astype(jnp.int32)
            return result

        block(*(pick([o[i] for o in ORDER]) for i in range(2)))

    c_send(4, 1, 0)
    for s in range(5):
        finish(s)
    for make in sent:
        make().wait_send()
    pltpu.make_async_copy(obuf, out_ref, os).wait()


def local(amplitudes, integrals, other_terms, of, os_, vf, vs, oe, ve):
    a = amplitudes.reshape(2, 8, 64, 128).transpose(0, 2, 1, 3).reshape(2, 2, 16, 2, 8, 128)
    b = integrals.reshape(4, 2, 128, 256)
    small = [v.reshape(1, -1) for v in (of, os_, vf, vs, oe)] + [ve]
    hbm = pl.BlockSpec(memory_space=pltpu.HBM)
    dma = pltpu.SemaphoreType.DMA
    return pl.pallas_call(
        kernel,
        out_shape=jax.ShapeDtypeStruct((512, 256), F32),
        in_specs=[hbm] * 9,
        out_specs=pl.BlockSpec(memory_space=pl.ANY),
        scratch_shapes=[
            pltpu.VMEM((8, 4, 2, 2, 16, 8, 128), F32),
            pltpu.VMEM((1024, 2048), BF16),
            pltpu.VMEM((1024, 2048), BF16),
            pltpu.VMEM((2, 4, 4, 128, 256), F32),
            pltpu.VMEM((2, 2048, 256), BF16),
            pltpu.VMEM((2, 2048, 256), BF16),
            pltpu.VMEM((2, 1024, 256), F32),
            pltpu.VMEM((3, 512, 256), F32),
            pltpu.VMEM((2, 8, 512), F32),
            pltpu.VMEM((2, 512, 128), F32),
            pltpu.VMEM((2, 8, 256), F32),
            pltpu.VMEM((512, 256), F32),
            *[pltpu.VMEM(v.shape, v.dtype) for v in small],
            dma((9,)), dma((28,)), dma((3,)), dma((18,)), dma((12,)), dma, dma((15,)), dma((2,)), dma, dma,
        ],
        compiler_params=pltpu.CompilerParams(
            collective_id=0, has_side_effects=True, vmem_limit_bytes=62 << 20
        ),
        cost_estimate=pl.CostEstimate(flops=6442450944, bytes_accessed=4 << 20, transcendentals=0),
    )(a, b, other_terms, *small)


def solution(mesh):
    in_specs = (
        P(("col", "row"), None),
        P("col", "row"),
        P("col", "row"),
        P("col"),
        P("col"),
        P("row"),
        P("row"),
        P(),
        P(),
    )
    return jax.shard_map(local, mesh=mesh, in_specs=in_specs, out_specs=P("col", "row"), check_vma=False)
```

```python
import jax
import jax.numpy as jnp
from jax import lax
from jax.experimental import pallas as pl
from jax.experimental.pallas import tpu as pltpu
from jax.sharding import PartitionSpec as P

MESH = pl.DeviceIdType.MESH
F32, BF16 = jnp.float32, jnp.bfloat16
START = (0, 64, 192, 320, 448, 512)
CHUNKS = ((0, 0, 256), (1, 0, 128), (1, 128, 128), (1, 0, 256))
ALL0, LOW1, HIGH1, ALL1 = range(4)
ORDER = (
    (0, 1, ALL0), (2, 2, ALL0), (6, 2, ALL0), (2, 2, LOW1), (0, 1, LOW1), (6, 2, LOW1), (12, 1, ALL0), (12, 1, LOW1),
    (2, 2, HIGH1), (6, 2, HIGH1), (0, 1, HIGH1), (12, 1, HIGH1), (15, 0, ALL1), (15, 0, ALL0), (10, 1, ALL1),
    (14, 0, ALL1), (14, 0, ALL0), (10, 1, ALL0),
)


def lookup(index_ref, table_ref):
    n = table_ref.shape[-1]
    onehot = (lax.broadcasted_iota(jnp.int32, (n, index_ref.shape[1]), 0) == index_ref[...]).astype(F32)
    table = jnp.broadcast_to(table_ref[...].reshape(1, n), (8, n))
    return jnp.dot(table, onehot, precision=lax.Precision.HIGHEST, preferred_element_type=F32)


def kernel(
    a_ref, b_ref, other_ref, *refs
):
    small, out_ref, refs = refs[:6], refs[6], refs[7:]
    abuf, ahi, alo, bbuf, bhi, blo, cbuf, rbuf, occ_row, occ_col, vsum, obuf = refs[:12]
    small_v, (loc, zr, xr, sr, yr, er, cr, tr, os, sends) = refs[12:18], refs[18:]
    of_ref, os_ref, vf_ref, vs_ref, oe_ref, ve_ref = small_v
    row, col = lax.axis_index("row"), lax.axis_index("col")
    xl, z, c = row // 16, (row // 2) % 8, row % 2
    xh, y = col // 4, col % 4

    def dev(xh, xl, y, z, c):
        return (xl * 16 + z * 2 + c, xh * 4 + y)

    px = ((xh, xl), (xh, 1 - xl), (1 - xh, 1 - xl), (1 - xh, xl))
    xi = [h * 2 + l for h, l in px]
    xdev = [dev(h, l, y, z, c) for h, l in px]
    zp, zm = (z + 1) % 8, (z + 7) % 8
    yp, ym, y2 = (y + 1) % 4, (y + 3) % 4, (y + 2) % 4
    zdev = (dev(xh, xl, y, zp, c), dev(xh, xl, y, zm, c))
    ydev = (dev(xh, xl, yp, z, c), dev(xh, xl, ym, z, c))
    sib = dev(xh, xl, y, z, 1 - c)

    def sides(s):
        return range(1 if s in (0, 4) else 2)

    zs_of = [((z + 8 - s) % 8, (z + s) % 8) for s in range(5)]

    def zof(s, p):
        return zs_of[s][p]

    def remote(src, dst, recv, to):
        return pltpu.make_async_remote_copy(
            src_ref=src, dst_ref=dst, send_sem=sends, recv_sem=recv, device_id=to, device_id_type=MESH
        )

    sent = []

    def go(make):
        make().start()
        sent.append(make)

    barrier = pltpu.get_barrier_semaphore()
    for to in (*xdev[1:], *zdev, *ydev, sib):
        pl.semaphore_signal(barrier, inc=1, device_id=to, device_id_type=MESH)
    local = [pltpu.make_async_copy(src, dst, loc.at[i]) for i, (src, dst) in enumerate(zip(small, small_v))]
    own_a = pltpu.make_async_copy(a_ref.at[:, xh, :, xl], abuf.at[z, xi[0], c], loc.at[6])
    own_b = pltpu.make_async_copy(b_ref.at[:, xl], bbuf.at[0, y], loc.at[7])
    own_o = pltpu.make_async_copy(other_ref, obuf, loc.at[8])
    for copy in (own_a, *local, own_b, own_o):
        copy.start()

    def arrive(at, recv):
        remote(at, at, recv, sib).wait_recv()

    def z_sem(s, q, d):
        return zr.at[(s - 1) * 8 + d * 4 + q if s < 4 else 24 + q]

    def z_send(s, q, d):
        def make():
            where = abuf.at[zof(s, d), xi[q], c]
            src = a_ref.at[:, xh, :, xl] if s == 0 and q == 0 else where
            return remote(src, where, z_sem(s + 1, q, d), zdev[d])

        go(make)

    def z_wait(s, q):
        for d in range(2):
            if s < 4 or d == q % 2:
                arrive(abuf.at[zof(s, d), xi[q], c], z_sem(s, q, d))

    def z_forward(s, q):
        for d in range(2):
            if s < 3 or d == q % 2:
                z_send(s, q, d)

    def z_step(s, q):
        for d in (q % 2, 1 - q % 2):
            arrive(abuf.at[zof(s, d), xi[q], c], z_sem(s, q, d))
            if s < 3 or d == q % 2:
                z_send(s, q, d)

    def x_send(q):
        go(lambda: remote(a_ref.at[:, px[q][0], :, px[q][1]], abuf.at[z, xi[0], c], xr.at[q - 1], xdev[q]))

    def x_step(q):
        arrive(abuf.at[z, xi[q], c], xr.at[q - 1])
        for d in range(2):
            z_send(0, q, d)

    def sib_at(s, p, k, core):
        if s == 4:
            return abuf.at[zof(s, 0), xi[k], core], sr.at[14 + k]
        where = abuf.at[zof(s, p), pl.ds(2 * (xh if k == 0 else 1 - xh), 2), core]
        return where, sr.at[2 * (0 if s == 0 else 2 * s - 1 + p) + k]

    def sib_send(s, k):
        for p in sides(s):

            def make(p=p):
                where, sem = sib_at(s, p, k, c)
                return remote(where, where, sem, sib)

            go(make)

    def sib_wait(s, k):
        for p in sides(s):
            arrive(*sib_at(s, p, k, 1 - c))

    def b_at(n, yy, groups=slice(None)):
        h, l0, nl = CHUNKS[n]
        return bbuf.at[h, yy, groups, :, l0 : l0 + nl]

    def part(i, d):
        return pl.ds(2 * (i if d == 0 else 1 - i), 2)

    def y_send(n, i):
        h, l0, nl = CHUNKS[n]
        for d in range(2):

            def make(d=d):
                src = b_ref.at[part(i, d), xl, :, l0 : l0 + nl] if h == 0 else b_at(n, y, part(i, d))
                return remote(src, b_at(n, y, part(i, d)), yr.at[n * 6 + i * 2 + d], ydev[d])

            go(make)

    def y_wait(n, i):
        for d in range(2):
            arrive(b_at(n, (ym, yp)[d], part(i, d)), yr.at[n * 6 + i * 2 + d])

    def y_forward(n):
        for d in range(2):

            def make(d=d):
                at = b_at(n, (ym, yp)[d], part(0, d))
                return remote(at, at, yr.at[n * 6 + 4 + d], ydev[d])

            go(make)

    def y_far(n):
        for d in range(2):
            arrive(b_at(n, y2, part(0, d)), yr.at[n * 6 + 4 + d])

    def e_send(n):
        h, l0, nl = CHUNKS[n]
        go(lambda: remote(b_ref.at[:, 1 - xl, :, l0 : l0 + nl], b_at(n, y), er.at[n - LOW1], xdev[1]))

    def e_wait(n):
        arrive(b_at(n, y), er.at[n - LOW1])

    def split_b(n, yy):
        h, l0, nl = CHUNKS[n]
        lanes = slice(l0, l0 + nl)

        @pl.loop(0, 16)
        def _(i):
            g, r = i // 4, pl.multiple_of((i % 4) * 32, 32)
            v = bbuf[h, yy, g, pl.ds(r, 32), lanes]
            hi = v.astype(BF16)
            to = pl.ds(pl.multiple_of(yy * 512 + g * 128 + r, 32), 32)
            bhi[h, to, lanes] = hi
            blo[h, to, lanes] = (v - hi.astype(F32)).astype(BF16)

    def rows_at(s, p, k):
        return (64 * k if s in (0, 4) else 128 * k - 128) + 256 * s - (128 if s == 4 else 0) + 64 * p

    def split_a(s, k):
        @pl.loop(0, 16)
        def _(j):
            lanes = pl.ds(pl.multiple_of(j * 128, 128), 128)
            for p in sides(s):
                v = abuf[zof(s, p), pl.ds(2 * (xh if k == 0 else 1 - xh), 2), :, :, j].reshape(64, 128)
                hi = v.astype(BF16)
                r = rows_at(s, p, k)
                ahi[r : r + 64, lanes] = hi
                alo[r : r + 64, lanes] = (v - hi.astype(F32)).astype(BF16)

    mine = z * 2 + c
    panel_h = jnp.where(xh == xl, 0, 1)

    def block(first, scale, n):
        h = (n != ALL0).astype(jnp.int32)
        low, high = n != HIGH1, n != LOW1
        r0 = pl.multiple_of(first * 64, 64)

        def product(size):
            rows = pl.ds(r0, size)
            total = (
                jnp.dot(alo[rows, :], bhi[h], preferred_element_type=F32)
                + jnp.dot(ahi[rows, :], blo[h], preferred_element_type=F32)
                + jnp.dot(ahi[rows, :], bhi[h], preferred_element_type=F32)
            )

            @pl.when(low)
            def _():
                cbuf[h, rows, :128] = total[:, :128]

            @pl.when(high)
            def _():
                cbuf[h, rows, 128:] = total[:, 128:]

        for k in range(3):
            pl.when(scale == k)(lambda k=k: product(64 << k))

        @pl.when((panel_h == h) & ((low & (xl == 0)) | (high & (xl == 1))))
        def _():
            lanes = pl.ds(pl.multiple_of(xl * 128, 128), 128)

            @pl.loop(0, 2 + 2 * scale + 2 * (scale // 2))
            def _(i):
                bb, g = (2 * first + i) // 4, (2 * first + i) % 4
                s, both = (bb + 1) // 2, ((bb == 0) | (bb == 7)).astype(jnp.int32)
                k = both * (g // 2) + (1 - both) * ((bb + 1) % 2)
                up = (1 - both) * (g // 2)
                zz = (z + 8 + (2 * up - 1) * s) % 8
                x = 2 * (xh + k - 2 * xh * k) + g % 2
                v = abuf[zz, x, :, :, mine].reshape(32, 128)
                o = occ_col[k, pl.ds(pl.multiple_of(g % 2 * 256 + zz * 32, 32), 32), :]
                cbuf[h, pl.ds(pl.multiple_of(r0 + 32 * i, 32), 32), lanes] += v * (vsum[h, 0:1, lanes] - o)

    def c_copy(s, k, n):
        h, l0, nl = CHUNKS[n]
        q = 3 if h == 0 else 1 + k
        size, lanes = START[s + 1] - START[s], slice(l0, l0 + nl)
        src = cbuf.at[h, rows_at(s, 0, k) : rows_at(s, 0, k) + size, lanes]
        dst = rbuf.at[q - 1, START[s] : START[s] + size, lanes]
        return remote(src, dst, cr.at[s * 6 + 2 * (q - 1) + (1 if l0 else 0)], xdev[q])

    c_sent = []

    def c_send(*what):
        go(lambda: c_copy(*what))
        c_sent.append(what)

    def finish(s):
        for what in c_sent:
            if what[0] == s:
                c_copy(*what).wait_recv()
        for p in sides(s):
            zz = zof(s, p)
            for l in range(2):
                r, t = rows_at(s, p, 0) + l * 32, START[s] + p * 64 + l * 32
                here, there = slice(r, r + 32), slice(t, t + 32)
                at = pl.ds(pl.multiple_of(l * 256 + zz * 32, 32), 32)
                total = (cbuf[0, here, :] + rbuf[2, there, :]) + (rbuf[0, there, :] + rbuf[1, there, :])
                o = occ_col[0, at, :]
                d = vsum[0, 0:1, :] - jnp.concatenate([o, o], axis=1)
                obuf[at, :] = (obuf[at, :] + total) / d
                pltpu.make_async_copy(obuf.at[at], out_ref.at[at], os).start()

    pl.semaphore_wait(barrier, 8)
    for d in range(2):
        z_send(0, 0, d)
    for q in (1, 2, 3):
        x_send(q)
    y_send(ALL0, 0)
    y_send(ALL0, 1)
    for copy in local:
        copy.wait()
    occ_row[0] = lookup(of_ref, oe_ref) + lookup(os_ref, oe_ref)
    vsum[0] = lookup(vf_ref, ve_ref) + lookup(vs_ref, ve_ref)
    go(lambda: remote(occ_row.at[0], occ_row.at[1], tr.at[0], xdev[3]))
    go(lambda: remote(vsum.at[0], vsum.at[1], tr.at[1], xdev[1]))
    e_send(LOW1)
    e_send(HIGH1)
    z_step(1, 0)
    x_step(2)
    x_step(1)
    y_wait(ALL0, 0)
    y_forward(ALL0)
    own_b.wait()
    split_b(ALL0, y)
    x_step(3)
    own_a.wait()
    sib_send(0, 0)
    sib_send(0, 1)
    z_step(1, 2)
    e_wait(LOW1)
    y_send(LOW1, 0)
    y_send(LOW1, 1)
    occ_col[0] = jnp.broadcast_to(occ_row[0, 0:1, :], (128, 512)).T
    arrive(occ_row.at[1], tr.at[0])
    arrive(vsum.at[1], tr.at[1])
    occ_col[1] = jnp.broadcast_to(occ_row[1, 0:1, :], (128, 512)).T
    y_wait(ALL0, 1)
    split_b(ALL0, ym)
    split_b(ALL0, yp)
    z_step(1, 1)
    for k in range(2):
        sib_wait(0, k)
        split_a(0, k)
    split_b(LOW1, y)
    z_step(1, 3)
    sib_send(1, 1)
    sib_send(1, 0)
    y_far(ALL0)
    split_b(ALL0, y2)
    z_step(2, 2)

    before = [[] for _ in ORDER]

    def at(j, f, *a):
        before[j].append(lambda: f(*a))

    at(1, c_send, 0, 1, ALL0)
    at(1, sib_wait, 1, 1)
    at(1, split_a, 1, 1)
    at(1, sib_wait, 1, 0)
    at(1, split_a, 1, 0)
    at(1, y_wait, LOW1, 0)
    at(1, y_forward, LOW1)
    at(1, e_wait, HIGH1)
    at(1, y_send, HIGH1, 0)
    at(1, y_send, HIGH1, 1)
    at(1, split_b, HIGH1, y)
    at(2, c_send, 1, 1, ALL0)
    at(2, z_step, 2, 3)
    at(2, sib_send, 2, 1)
    at(2, z_wait, 2, 0)
    at(2, z_step, 2, 1)
    at(2, sib_send, 2, 0)
    at(2, y_wait, LOW1, 1)
    at(2, split_b, LOW1, ym)
    at(2, split_b, LOW1, yp)
    at(2, sib_wait, 2, 1)
    at(2, split_a, 2, 1)
    at(2, sib_wait, 2, 0)
    at(2, split_a, 2, 0)
    at(3, c_send, 2, 1, ALL0)
    at(3, y_far, LOW1)
    at(3, split_b, LOW1, y2)
    at(4, c_send, 1, 0, LOW1)
    at(4, c_send, 1, 1, LOW1)
    at(4, z_step, 3, 2)
    at(5, c_send, 0, 0, LOW1)
    at(5, c_send, 0, 1, LOW1)
    at(6, c_send, 2, 0, LOW1)
    at(6, c_send, 2, 1, LOW1)
    at(6, y_wait, HIGH1, 0)
    at(6, y_forward, HIGH1)
    at(6, z_step, 3, 3)
    at(6, z_forward, 2, 0)
    at(6, sib_send, 3, 1)
    at(6, sib_wait, 3, 1)
    at(6, split_a, 3, 1)
    at(7, c_send, 3, 1, ALL0)
    at(7, z_step, 3, 1)
    at(8, c_send, 3, 1, LOW1)
    at(8, y_wait, HIGH1, 1)
    at(8, split_b, HIGH1, ym)
    at(8, split_b, HIGH1, yp)
    at(8, y_far, HIGH1)
    at(8, split_b, HIGH1, y2)
    at(9, c_send, 1, 0, HIGH1)
    at(9, c_send, 1, 1, HIGH1)
    for q in (2, 3):
        at(9, z_wait, 4, q)
        at(9, sib_send, 4, q)
    at(10, c_send, 2, 0, HIGH1)
    at(10, c_send, 2, 1, HIGH1)
    at(11, c_send, 0, 0, HIGH1)
    at(11, c_send, 0, 1, HIGH1)
    at(11, z_step, 3, 0)
    at(11, sib_send, 3, 0)
    at(12, c_send, 3, 1, HIGH1)
    for q in (2, 3):
        at(12, sib_wait, 4, q)
    at(12, split_a, 4, 1)
    at(13, c_send, 4, 1, ALL1)
    at(14, c_send, 4, 1, ALL0)
    at(14, sib_wait, 3, 0)
    at(14, split_a, 3, 0)
    at(15, c_send, 3, 0, ALL1)
    for q in (0, 1):
        at(15, z_wait, 4, q)
        at(15, sib_send, 4, q)
    at(15, own_o.wait)
    for q in (0, 1):
        at(15, sib_wait, 4, q)
    at(15, split_a, 4, 0)
    at(16, c_send, 4, 0, ALL1)

    @pl.loop(0, len(ORDER))
    def _(j):
        def run(first, end):
            if end - first == 1:
                for step in before[first]:
                    step()
            else:
                middle = (first + end) // 2
                pl.when(j < middle)(lambda: run(first, middle))
                pl.when(j >= middle)(lambda: run(middle, end))

        run(0, len(ORDER))

        def pick(values):
            result = values[0]
            for i in range(1, len(values)):
                if values[i] != values[i - 1]:
                    result += (values[i] - values[i - 1]) * (j >= i).astype(jnp.int32)
            return result

        block(*(pick([o[i] for o in ORDER]) for i in range(3)))

    for s in range(5):
        finish(s)
    for make in sent:
        make().wait_send()
    pltpu.make_async_copy(obuf, out_ref, os).wait()


def local(amplitudes, integrals, other_terms, of, os_, vf, vs, oe, ve):
    a = amplitudes.reshape(2, 8, 64, 128).transpose(0, 2, 1, 3).reshape(2, 2, 16, 2, 8, 128)
    b = integrals.reshape(4, 2, 128, 256)
    small = [v.reshape(1, -1) for v in (of, os_, vf, vs, oe)] + [ve]
    hbm = pl.BlockSpec(memory_space=pltpu.HBM)
    dma = pltpu.SemaphoreType.DMA
    return pl.pallas_call(
        kernel,
        out_shape=jax.ShapeDtypeStruct((512, 256), F32),
        in_specs=[hbm] * 9,
        out_specs=pl.BlockSpec(memory_space=pl.ANY),
        scratch_shapes=[
            pltpu.VMEM((8, 4, 2, 2, 16, 8, 128), F32),
            pltpu.VMEM((1024, 2048), BF16),
            pltpu.VMEM((1024, 2048), BF16),
            pltpu.VMEM((2, 4, 4, 128, 256), F32),
            pltpu.VMEM((2, 2048, 256), BF16),
            pltpu.VMEM((2, 2048, 256), BF16),
            pltpu.VMEM((2, 1024, 256), F32),
            pltpu.VMEM((3, 512, 256), F32),
            pltpu.VMEM((2, 8, 512), F32),
            pltpu.VMEM((2, 512, 128), F32),
            pltpu.VMEM((2, 8, 256), F32),
            pltpu.VMEM((512, 256), F32),
            *[pltpu.VMEM(v.shape, v.dtype) for v in small],
            dma((9,)), dma((28,)), dma((3,)), dma((18,)), dma((18,)), dma((2,)), dma((30,)), dma((2,)), dma, dma,
        ],
        compiler_params=pltpu.CompilerParams(
            collective_id=0, has_side_effects=True, vmem_limit_bytes=62 << 20
        ),
        cost_estimate=pl.CostEstimate(flops=6442450944, bytes_accessed=4 << 20, transcendentals=0),
    )(a, b, other_terms, *small)


def solution(mesh):
    in_specs = (
        P(("col", "row"), None),
        P("col", "row"),
        P("col", "row"),
        P("col"),
        P("col"),
        P("row"),
        P("row"),
        P(),
        P(),
    )
    return jax.shard_map(local, mesh=mesh, in_specs=in_specs, out_specs=P("col", "row"), check_vma=False)
```

```python
import jax
import jax.numpy as jnp
from jax import lax
from jax.experimental import pallas as pl
from jax.experimental.pallas import tpu as pltpu
from jax.sharding import PartitionSpec as P

MESH = pl.DeviceIdType.MESH
F32, BF16 = jnp.float32, jnp.bfloat16
START = (0, 64, 192, 320, 448, 512)
CHUNKS = ((0, 0, 256), (1, 0, 128), (1, 128, 128), (1, 0, 256))
ALL0, LOW1, HIGH1, ALL1 = range(4)
ORDER = (
    (0, 1, ALL0), (2, 2, ALL0), (2, 2, LOW1), (0, 1, LOW1), (6, 2, ALL0), (6, 2, LOW1), (12, 1, ALL0),
    (2, 2, HIGH1), (6, 2, HIGH1), (0, 1, HIGH1), (12, 1, ALL1), (15, 0, ALL0), (10, 1, ALL1), (15, 0, ALL1),
    (14, 0, ALL1), (10, 1, ALL0), (14, 0, ALL0),
)


def lookup(index_ref, table_ref):
    n = table_ref.shape[-1]
    onehot = (lax.broadcasted_iota(jnp.int32, (n, index_ref.shape[1]), 0) == index_ref[...]).astype(F32)
    table = jnp.broadcast_to(table_ref[...].reshape(1, n), (8, n))
    return jnp.dot(table, onehot, precision=lax.Precision.HIGHEST, preferred_element_type=F32)


def kernel(
    a_ref, b_ref, other_ref, *refs
):
    small, out_ref, refs = refs[:6], refs[6], refs[7:]
    abuf, ahi, alo, bbuf, bhi, blo, cbuf, rbuf, occ_row, occ_col, vsum, obuf = refs[:12]
    small_v, (loc, zr, xr, sr, yr, er, cr, tr, os, sends) = refs[12:18], refs[18:]
    of_ref, os_ref, vf_ref, vs_ref, oe_ref, ve_ref = small_v
    row, col = lax.axis_index("row"), lax.axis_index("col")
    xl, z, c = row // 16, (row // 2) % 8, row % 2
    xh, y = col // 4, col % 4

    def dev(xh, xl, y, z, c):
        return (xl * 16 + z * 2 + c, xh * 4 + y)

    px = ((xh, xl), (xh, 1 - xl), (1 - xh, 1 - xl), (1 - xh, xl))
    xi = [h * 2 + l for h, l in px]
    xdev = [dev(h, l, y, z, c) for h, l in px]
    zp, zm = (z + 1) % 8, (z + 7) % 8
    yp, ym, y2 = (y + 1) % 4, (y + 3) % 4, (y + 2) % 4
    zdev = (dev(xh, xl, y, zp, c), dev(xh, xl, y, zm, c))
    ydev = (dev(xh, xl, yp, z, c), dev(xh, xl, ym, z, c))
    sib = dev(xh, xl, y, z, 1 - c)

    def sides(s):
        return range(1 if s in (0, 4) else 2)

    zs_of = [((z + 8 - s) % 8, (z + s) % 8) for s in range(5)]

    def zof(s, p):
        return zs_of[s][p]

    def remote(src, dst, recv, to):
        return pltpu.make_async_remote_copy(
            src_ref=src, dst_ref=dst, send_sem=sends, recv_sem=recv, device_id=to, device_id_type=MESH
        )

    sent = []

    def go(make):
        make().start()
        sent.append(make)

    barrier = pltpu.get_barrier_semaphore()
    for to in (*xdev[1:], *zdev, *ydev, sib):
        pl.semaphore_signal(barrier, inc=1, device_id=to, device_id_type=MESH)
    local = [pltpu.make_async_copy(src, dst, loc.at[i]) for i, (src, dst) in enumerate(zip(small, small_v))]
    own_a = pltpu.make_async_copy(a_ref.at[:, xh, :, xl], abuf.at[z, xi[0], c], loc.at[6])
    own_b = pltpu.make_async_copy(b_ref.at[:, xl], bbuf.at[0, y], loc.at[7])
    own_o = pltpu.make_async_copy(other_ref, obuf, loc.at[8])
    for copy in (own_a, *local, own_b, own_o):
        copy.start()

    def arrive(at, recv):
        remote(at, at, recv, sib).wait_recv()

    def z_sem(s, q, d):
        return zr.at[(s - 1) * 8 + d * 4 + q if s < 4 else 24 + q]

    def z_send(s, q, d):
        def make():
            where = abuf.at[zof(s, d), xi[q], c]
            src = a_ref.at[:, xh, :, xl] if s == 0 and q == 0 else where
            return remote(src, where, z_sem(s + 1, q, d), zdev[d])

        go(make)

    def z_wait(s, q, d):
        arrive(abuf.at[zof(s, d), xi[q], c], z_sem(s, q, d))

    def z_step(s, q):
        for d in (q % 2, 1 - q % 2):
            z_wait(s, q, d)
            if s < 3 or d == q % 2:
                z_send(s, q, d)

    def x_send(q):
        go(lambda: remote(a_ref.at[:, px[q][0], :, px[q][1]], abuf.at[z, xi[0], c], xr.at[q - 1], xdev[q]))

    def x_step(q):
        arrive(abuf.at[z, xi[q], c], xr.at[q - 1])
        for d in range(2):
            z_send(0, q, d)

    def sib_at(s, p, k, core):
        if s == 4:
            return abuf.at[zof(s, 0), xi[k], core], sr.at[14 + k]
        where = abuf.at[zof(s, p), pl.ds(2 * (xh if k == 0 else 1 - xh), 2), core]
        return where, sr.at[2 * (0 if s == 0 else 2 * s - 1 + p) + k]

    def sib_send(s, k):
        for p in sides(s):

            def make(p=p):
                where, sem = sib_at(s, p, k, c)
                return remote(where, where, sem, sib)

            go(make)

    def sib_wait(s, k):
        for p in sides(s):
            arrive(*sib_at(s, p, k, 1 - c))

    def b_at(n, yy, groups=slice(None)):
        h, l0, nl = CHUNKS[n]
        return bbuf.at[h, yy, groups, :, l0 : l0 + nl]

    def part(i, d):
        return pl.ds(2 * (i if d == 0 else 1 - i), 2)

    def y_send(n, i):
        h, l0, nl = CHUNKS[n]
        for d in range(2):

            def make(d=d):
                src = b_ref.at[part(i, d), xl, :, l0 : l0 + nl] if h == 0 else b_at(n, y, part(i, d))
                return remote(src, b_at(n, y, part(i, d)), yr.at[n * 6 + i * 2 + d], ydev[d])

            go(make)

    def y_wait(n, i):
        for d in range(2):
            arrive(b_at(n, (ym, yp)[d], part(i, d)), yr.at[n * 6 + i * 2 + d])

    def y_forward(n):
        for d in range(2):

            def make(d=d):
                at = b_at(n, (ym, yp)[d], part(0, d))
                return remote(at, at, yr.at[n * 6 + 4 + d], ydev[d])

            go(make)

    def y_far(n):
        for d in range(2):
            arrive(b_at(n, y2, part(0, d)), yr.at[n * 6 + 4 + d])

    def e_send(n):
        h, l0, nl = CHUNKS[n]
        go(lambda: remote(b_ref.at[:, 1 - xl, :, l0 : l0 + nl], b_at(n, y), er.at[n - LOW1], xdev[1]))

    def e_wait(n):
        arrive(b_at(n, y), er.at[n - LOW1])

    def split_b(n, yy):
        h, l0, nl = CHUNKS[n]
        lanes = slice(l0, l0 + nl)

        @pl.loop(0, 16)
        def _(i):
            g, r = i // 4, pl.multiple_of((i % 4) * 32, 32)
            v = bbuf[h, yy, g, pl.ds(r, 32), lanes]
            hi = v.astype(BF16)
            to = pl.ds(pl.multiple_of(yy * 512 + g * 128 + r, 32), 32)
            bhi[h, to, lanes] = hi
            blo[h, to, lanes] = (v - hi.astype(F32)).astype(BF16)

    def rows_at(s, p, k):
        return (64 * k if s in (0, 4) else 128 * k - 128) + 256 * s - (128 if s == 4 else 0) + 64 * p

    def split_a(s, k):
        @pl.loop(0, 16)
        def _(j):
            lanes = pl.ds(pl.multiple_of(j * 128, 128), 128)
            for p in sides(s):
                v = abuf[zof(s, p), pl.ds(2 * (xh if k == 0 else 1 - xh), 2), :, :, j].reshape(64, 128)
                hi = v.astype(BF16)
                r = rows_at(s, p, k)
                ahi[r : r + 64, lanes] = hi
                alo[r : r + 64, lanes] = (v - hi.astype(F32)).astype(BF16)

    mine = z * 2 + c
    panel_h = jnp.where(xh == xl, 0, 1)

    def block(first, scale, n):
        h = (n != ALL0).astype(jnp.int32)
        low, high = n != HIGH1, n != LOW1
        r0 = pl.multiple_of(first * 64, 64)

        def product(size):
            rows = pl.ds(r0, size)
            total = (
                jnp.dot(alo[rows, :], bhi[h], preferred_element_type=F32)
                + jnp.dot(ahi[rows, :], blo[h], preferred_element_type=F32)
                + jnp.dot(ahi[rows, :], bhi[h], preferred_element_type=F32)
            )

            @pl.when(low)
            def _():
                cbuf[h, rows, :128] = total[:, :128]

            @pl.when(high)
            def _():
                cbuf[h, rows, 128:] = total[:, 128:]

        for k in range(3):
            pl.when(scale == k)(lambda k=k: product(64 << k))

        @pl.when((panel_h == h) & ((low & (xl == 0)) | (high & (xl == 1))))
        def _():
            lanes = pl.ds(pl.multiple_of(xl * 128, 128), 128)

            @pl.loop(0, 2 + 2 * scale + 2 * (scale // 2))
            def _(i):
                bb, g = (2 * first + i) // 4, (2 * first + i) % 4
                s, both = (bb + 1) // 2, ((bb == 0) | (bb == 7)).astype(jnp.int32)
                k = both * (g // 2) + (1 - both) * ((bb + 1) % 2)
                up = (1 - both) * (g // 2)
                zz = (z + 8 + (2 * up - 1) * s) % 8
                x = 2 * (xh + k - 2 * xh * k) + g % 2
                v = abuf[zz, x, :, :, mine].reshape(32, 128)
                o = occ_col[k, pl.ds(pl.multiple_of(g % 2 * 256 + zz * 32, 32), 32), :]
                cbuf[h, pl.ds(pl.multiple_of(r0 + 32 * i, 32), 32), lanes] += v * (vsum[h, 0:1, lanes] - o)

    def c_copy(s, k, n):
        h, l0, nl = CHUNKS[n]
        q = 3 if h == 0 else 1 + k
        size, lanes = START[s + 1] - START[s], slice(l0, l0 + nl)
        src = cbuf.at[h, rows_at(s, 0, k) : rows_at(s, 0, k) + size, lanes]
        dst = rbuf.at[q - 1, START[s] : START[s] + size, lanes]
        return remote(src, dst, cr.at[s * 6 + 2 * (q - 1) + (1 if l0 else 0)], xdev[q])

    c_sent = []

    def c_send(*what):
        go(lambda: c_copy(*what))
        c_sent.append(what)

    def finish(s):
        for what in c_sent:
            if what[0] == s:
                c_copy(*what).wait_recv()
        for p in sides(s):
            zz = zof(s, p)
            for l in range(2):
                r, t = rows_at(s, p, 0) + l * 32, START[s] + p * 64 + l * 32
                here, there = slice(r, r + 32), slice(t, t + 32)
                at = pl.ds(pl.multiple_of(l * 256 + zz * 32, 32), 32)
                total = (cbuf[0, here, :] + rbuf[2, there, :]) + (rbuf[0, there, :] + rbuf[1, there, :])
                o = occ_col[0, at, :]
                d = vsum[0, 0:1, :] - jnp.concatenate([o, o], axis=1)
                obuf[at, :] = (obuf[at, :] + total) / d
                pltpu.make_async_copy(obuf.at[at], out_ref.at[at], os).start()

    pl.semaphore_wait(barrier, 8)
    for d in range(2):
        z_send(0, 0, d)
    for q in (1, 2, 3):
        x_send(q)
    y_send(ALL0, 0)
    y_send(ALL0, 1)
    for copy in local:
        copy.wait()
    occ_row[0] = lookup(of_ref, oe_ref) + lookup(os_ref, oe_ref)
    vsum[0] = lookup(vf_ref, ve_ref) + lookup(vs_ref, ve_ref)
    go(lambda: remote(occ_row.at[0], occ_row.at[1], tr.at[0], xdev[3]))
    go(lambda: remote(vsum.at[0], vsum.at[1], tr.at[1], xdev[1]))
    e_send(LOW1)
    e_send(HIGH1)
    z_step(1, 0)
    x_step(2)
    x_step(1)
    y_wait(ALL0, 0)
    y_forward(ALL0)
    own_b.wait()
    split_b(ALL0, y)
    x_step(3)
    own_a.wait()
    sib_send(0, 0)
    sib_send(0, 1)
    z_step(1, 2)
    e_wait(LOW1)
    y_send(LOW1, 0)
    y_send(LOW1, 1)
    occ_col[0] = jnp.broadcast_to(occ_row[0, 0:1, :], (128, 512)).T
    arrive(occ_row.at[1], tr.at[0])
    arrive(vsum.at[1], tr.at[1])
    occ_col[1] = jnp.broadcast_to(occ_row[1, 0:1, :], (128, 512)).T
    y_wait(ALL0, 1)
    split_b(ALL0, ym)
    split_b(ALL0, yp)
    z_step(1, 1)
    for k in range(2):
        sib_wait(0, k)
        split_a(0, k)
    split_b(LOW1, y)
    z_step(1, 3)
    sib_send(1, 1)
    sib_send(1, 0)
    y_far(ALL0)
    split_b(ALL0, y2)
    z_step(2, 2)

    before = [[] for _ in ORDER]

    def at(j, f, *a):
        before[j].append(lambda: f(*a))

    at(1, c_send, 0, 1, ALL0)
    at(1, sib_wait, 1, 1)
    at(1, split_a, 1, 1)
    at(1, sib_wait, 1, 0)
    at(1, split_a, 1, 0)
    at(1, y_wait, LOW1, 0)
    at(1, y_forward, LOW1)
    at(1, e_wait, HIGH1)
    at(1, y_send, HIGH1, 0)
    at(1, y_send, HIGH1, 1)
    at(1, split_b, HIGH1, y)
    at(2, c_send, 1, 1, ALL0)
    at(2, z_step, 2, 3)
    at(2, sib_send, 2, 1)
    for q in (0, 1):
        for d in (0, 1):
            at(2, z_wait, 2, q, d)
        at(2, z_send, 2, q, q)
    at(2, sib_send, 2, 0)
    at(2, y_wait, LOW1, 1)
    at(2, split_b, LOW1, ym)
    at(2, split_b, LOW1, yp)
    at(2, y_far, LOW1)
    at(2, split_b, LOW1, y2)
    at(3, c_send, 1, 0, LOW1)
    at(3, c_send, 1, 1, LOW1)
    at(4, c_send, 0, 0, LOW1)
    at(4, c_send, 0, 1, LOW1)
    at(4, z_step, 3, 2)
    at(4, sib_wait, 2, 1)
    at(4, split_a, 2, 1)
    at(4, sib_wait, 2, 0)
    at(4, split_a, 2, 0)
    at(5, c_send, 2, 1, ALL0)
    at(5, y_wait, HIGH1, 0)
    at(5, y_forward, HIGH1)
    at(6, c_send, 2, 0, LOW1)
    at(6, c_send, 2, 1, LOW1)
    at(6, z_step, 3, 3)
    for q in (0, 1):
        at(6, z_send, 2, q, 1 - q)
    at(6, sib_send, 3, 1)
    at(6, sib_wait, 3, 1)
    at(6, split_a, 3, 1)
    at(7, c_send, 3, 1, ALL0)
    for q in (0, 1):
        at(7, z_wait, 3, q, q)
        at(7, z_send, 3, q, q)
    at(7, y_wait, HIGH1, 1)
    at(7, split_b, HIGH1, ym)
    at(7, split_b, HIGH1, yp)
    at(7, y_far, HIGH1)
    at(7, split_b, HIGH1, y2)
    at(8, c_send, 1, 0, HIGH1)
    at(8, c_send, 1, 1, HIGH1)
    for q in (2, 3):
        at(8, z_wait, 4, q, q % 2)
        at(8, sib_send, 4, q)
    at(9, c_send, 2, 0, HIGH1)
    at(9, c_send, 2, 1, HIGH1)
    at(10, c_send, 0, 0, HIGH1)
    at(10, c_send, 0, 1, HIGH1)
    for q in (0, 1):
        at(10, z_wait, 3, q, 1 - q)
    at(10, sib_send, 3, 0)
    at(11, c_send, 3, 1, ALL1)
    for q in (2, 3):
        at(11, sib_wait, 4, q)
    at(11, split_a, 4, 1)
    at(12, c_send, 4, 1, ALL0)
    at(12, sib_wait, 3, 0)
    at(12, split_a, 3, 0)
    at(13, c_send, 3, 0, ALL1)
    for q in (0, 1):
        at(13, z_wait, 4, q, q)
        at(13, sib_send, 4, q)
    at(14, c_send, 4, 1, ALL1)
    at(14, own_o.wait)
    for q in (0, 1):
        at(14, sib_wait, 4, q)
    at(14, split_a, 4, 0)
    at(15, c_send, 4, 0, ALL1)

    @pl.loop(0, len(ORDER))
    def _(j):
        def run(first, end):
            if end - first == 1:
                for step in before[first]:
                    step()
            else:
                middle = (first + end) // 2
                pl.when(j < middle)(lambda: run(first, middle))
                pl.when(j >= middle)(lambda: run(middle, end))

        run(0, len(ORDER))

        def pick(values):
            result = values[0]
            for i in range(1, len(values)):
                if values[i] != values[i - 1]:
                    result += (values[i] - values[i - 1]) * (j >= i).astype(jnp.int32)
            return result

        block(*(pick([o[i] for o in ORDER]) for i in range(3)))

    for s in range(5):
        finish(s)
    for make in sent:
        make().wait_send()
    pltpu.make_async_copy(obuf, out_ref, os).wait()


def local(amplitudes, integrals, other_terms, of, os_, vf, vs, oe, ve):
    a = amplitudes.reshape(2, 8, 64, 128).transpose(0, 2, 1, 3).reshape(2, 2, 16, 2, 8, 128)
    b = integrals.reshape(4, 2, 128, 256)
    small = [v.reshape(1, -1) for v in (of, os_, vf, vs, oe)] + [ve]
    hbm = pl.BlockSpec(memory_space=pltpu.HBM)
    dma = pltpu.SemaphoreType.DMA
    return pl.pallas_call(
        kernel,
        out_shape=jax.ShapeDtypeStruct((512, 256), F32),
        in_specs=[hbm] * 9,
        out_specs=pl.BlockSpec(memory_space=pl.ANY),
        scratch_shapes=[
            pltpu.VMEM((8, 4, 2, 2, 16, 8, 128), F32),
            pltpu.VMEM((1024, 2048), BF16),
            pltpu.VMEM((1024, 2048), BF16),
            pltpu.VMEM((2, 4, 4, 128, 256), F32),
            pltpu.VMEM((2, 2048, 256), BF16),
            pltpu.VMEM((2, 2048, 256), BF16),
            pltpu.VMEM((2, 1024, 256), F32),
            pltpu.VMEM((3, 512, 256), F32),
            pltpu.VMEM((2, 8, 512), F32),
            pltpu.VMEM((2, 512, 128), F32),
            pltpu.VMEM((2, 8, 256), F32),
            pltpu.VMEM((512, 256), F32),
            *[pltpu.VMEM(v.shape, v.dtype) for v in small],
            dma((9,)), dma((28,)), dma((3,)), dma((18,)), dma((18,)), dma((2,)), dma((30,)), dma((2,)), dma, dma,
        ],
        compiler_params=pltpu.CompilerParams(
            collective_id=0, has_side_effects=True, vmem_limit_bytes=213 << 18
        ),
        cost_estimate=pl.CostEstimate(flops=6442450944, bytes_accessed=4 << 20, transcendentals=0),
    )(a, b, other_terms, *small)


def solution(mesh):
    in_specs = (
        P(("col", "row"), None),
        P("col", "row"),
        P("col", "row"),
        P("col"),
        P("col"),
        P("row"),
        P("row"),
        P(),
        P(),
    )
    return jax.shard_map(local, mesh=mesh, in_specs=in_specs, out_specs=P("col", "row"), check_vma=False)
```

```python
import jax
import jax.numpy as jnp
from jax import lax
from jax.experimental import pallas as pl
from jax.experimental.pallas import tpu as pltpu
from jax.sharding import PartitionSpec as P

MESH = pl.DeviceIdType.MESH
F32, BF16 = jnp.float32, jnp.bfloat16
START = (0, 64, 192, 320, 448, 512)
CHUNKS = ((0, 0, 256), (1, 0, 128), (1, 128, 128), (1, 0, 256))
ALL0, LOW1, HIGH1, ALL1 = range(4)
ROWS = (64, 128, 256, 384)
ORDER = (
    (0, 3, ALL0), (8, 1, ALL0), (0, 3, LOW1), (6, 2, LOW1), (6, 1, ALL0), (12, 1, ALL0),
    (0, 3, HIGH1), (6, 2, HIGH1), (12, 1, ALL1), (15, 0, ALL0), (10, 1, ALL1), (15, 0, ALL1),
    (14, 0, ALL1), (10, 1, ALL0), (14, 0, ALL0),
)


def lookup(index_ref, table_ref):
    n = table_ref.shape[-1]
    onehot = (lax.broadcasted_iota(jnp.int32, (n, index_ref.shape[1]), 0) == index_ref[...]).astype(F32)
    table = jnp.broadcast_to(table_ref[...].reshape(1, n), (8, n))
    return jnp.dot(table, onehot, precision=lax.Precision.HIGHEST, preferred_element_type=F32)


def kernel(
    a_ref, b_ref, other_ref, *refs
):
    small, out_ref, refs = refs[:6], refs[6], refs[7:]
    abuf, ahi, alo, bbuf, bhi, blo, cbuf, rbuf, occ_row, occ_col, vsum, obuf = refs[:12]
    small_v, (loc, zr, xr, sr, yr, er, cr, tr, os, sends) = refs[12:18], refs[18:]
    of_ref, os_ref, vf_ref, vs_ref, oe_ref, ve_ref = small_v
    row, col = lax.axis_index("row"), lax.axis_index("col")
    xl, z, c = row // 16, (row // 2) % 8, row % 2
    xh, y = col // 4, col % 4

    def dev(xh, xl, y, z, c):
        return (xl * 16 + z * 2 + c, xh * 4 + y)

    px = ((xh, xl), (xh, 1 - xl), (1 - xh, 1 - xl), (1 - xh, xl))
    xi = [h * 2 + l for h, l in px]
    xdev = [dev(h, l, y, z, c) for h, l in px]
    zp, zm = (z + 1) % 8, (z + 7) % 8
    yp, ym, y2 = (y + 1) % 4, (y + 3) % 4, (y + 2) % 4
    zdev = (dev(xh, xl, y, zp, c), dev(xh, xl, y, zm, c))
    ydev = (dev(xh, xl, yp, z, c), dev(xh, xl, ym, z, c))
    sib = dev(xh, xl, y, z, 1 - c)

    def sides(s):
        return range(1 if s in (0, 4) else 2)

    zs_of = [((z + 8 - s) % 8, (z + s) % 8) for s in range(5)]

    def zof(s, p):
        return zs_of[s][p]

    def remote(src, dst, recv, to):
        return pltpu.make_async_remote_copy(
            src_ref=src, dst_ref=dst, send_sem=sends, recv_sem=recv, device_id=to, device_id_type=MESH
        )

    sent = []

    def go(make):
        make().start()
        sent.append(make)

    barrier = pltpu.get_barrier_semaphore()
    for to in (*xdev[1:], *zdev, *ydev, sib):
        pl.semaphore_signal(barrier, inc=1, device_id=to, device_id_type=MESH)
    local = [pltpu.make_async_copy(src, dst, loc.at[i]) for i, (src, dst) in enumerate(zip(small, small_v))]
    own_a = pltpu.make_async_copy(a_ref.at[:, xh, :, xl], abuf.at[z, xi[0], c], loc.at[6])
    own_b = pltpu.make_async_copy(b_ref.at[:, xl], bbuf.at[0, y], loc.at[7])
    own_o = pltpu.make_async_copy(other_ref, obuf, loc.at[8])
    for copy in (own_a, *local, own_b, own_o):
        copy.start()

    def arrive(at, recv):
        remote(at, at, recv, sib).wait_recv()

    def z_sem(s, q, d):
        if s == 1:
            return zr.at[2 * q + d]
        if s == 4:
            return zr.at[8 + q // 2]
        if q > 1:
            return zr.at[6 + 4 * (s - 2) + 2 * q + d]
        return zr.at[18 if s == 2 else 19 + (q + d) % 2]

    def z_send(s, q, d):
        def make():
            where = abuf.at[zof(s, d), xi[q], c]
            src = a_ref.at[:, xh, :, xl] if s == 0 and q == 0 else where
            return remote(src, where, z_sem(s + 1, q, d), zdev[d])

        go(make)

    def z_pair(s, q, d):
        at = abuf.at[zof(s, d), pl.ds(0, 2)] if s == 2 else abuf.at[zof(s, d), xi[q]]
        arrive(at, z_sem(s, q, d))

    def z_step(s, q):
        for d in (q % 2, 1 - q % 2):
            arrive(abuf.at[zof(s, d), xi[q], c], z_sem(s, q, d))
            if s < 3 or d == q % 2:
                z_send(s, q, d)

    def x_send(q):
        go(lambda: remote(a_ref.at[:, px[q][0], :, px[q][1]], abuf.at[z, xi[0], c], xr.at[q - 1], xdev[q]))

    def x_step(q):
        arrive(abuf.at[z, xi[q], c], xr.at[q - 1])
        for d in range(2):
            z_send(0, q, d)

    def sib_at(s, p, k, core):
        pair = pl.ds(2 * (xh if k == 0 else 1 - xh), 2)
        return abuf.at[zof(s, p), pair if s else slice(None), core]

    def sib_sem(s, k):
        return sr.at[0 if s == 0 else 2 * s - 1 + k]

    def sib_send(s, k):
        for p in sides(s):

            def make(p=p):
                where = sib_at(s, p, k, c)
                return remote(where, where, sib_sem(s, k), sib)

            go(make)

    def sib_quarter(q):
        def make():
            where = abuf.at[zof(4, 0), xi[q], c]
            return remote(where, where, sib_sem(4, q // 2), sib)

        go(make)

    def sib_wait(s, k):
        arrive(abuf.at[zof(s, 0), :, 1 - c] if s < 4 else sib_at(s, 0, k, 1 - c), sib_sem(s, k))

    def b_at(n, yy, groups=slice(None)):
        h, l0, nl = CHUNKS[n]
        return bbuf.at[h, yy, groups, :, l0 : l0 + nl]

    def part(i, d):
        return pl.ds(2 * (i if d == 0 else 1 - i), 2)

    def y_send(n, i):
        h, l0, nl = CHUNKS[n]
        for d in range(2):

            def make(d=d):
                src = b_ref.at[part(i, d), xl, :, l0 : l0 + nl] if h == 0 else b_at(n, y, part(i, d))
                return remote(src, b_at(n, y, part(i, d)), yr.at[n * 3 + i], ydev[d])

            go(make)

    def y_wait(n, i):
        arrive(b_at(n, ym), yr.at[n * 3 + i])

    def y_forward(n):
        for d in range(2):

            def make(d=d):
                at = b_at(n, (ym, yp)[d], part(0, d))
                return remote(at, at, yr.at[n * 3 + 2], ydev[d])

            go(make)

    def y_far(n):
        arrive(b_at(n, y2), yr.at[n * 3 + 2])

    def e_send(n):
        h, l0, nl = CHUNKS[n]
        go(lambda: remote(b_ref.at[:, 1 - xl, :, l0 : l0 + nl], b_at(n, y), er.at[n - LOW1], xdev[1]))

    def e_wait(n):
        arrive(b_at(n, y), er.at[n - LOW1])

    def split_b(n, yy):
        h, l0, nl = CHUNKS[n]
        lanes = slice(l0, l0 + nl)

        @pl.loop(0, 16)
        def _(i):
            g, r = i // 4, pl.multiple_of((i % 4) * 32, 32)
            v = bbuf[h, yy, g, pl.ds(r, 32), lanes]
            hi = v.astype(BF16)
            to = pl.ds(pl.multiple_of(yy * 512 + g * 128 + r, 32), 32)
            bhi[h, to, lanes] = hi
            blo[h, to, lanes] = (v - hi.astype(F32)).astype(BF16)

    def rows_at(s, p, k):
        return (64 * k if s in (0, 4) else 128 * k - 128) + 256 * s - (128 if s == 4 else 0) + 64 * p

    def split_a(s, k):
        @pl.loop(0, 16)
        def _(j):
            lanes = pl.ds(pl.multiple_of(j * 128, 128), 128)
            for p in sides(s):
                v = abuf[zof(s, p), pl.ds(2 * (xh if k == 0 else 1 - xh), 2), :, :, j].reshape(64, 128)
                hi = v.astype(BF16)
                r = rows_at(s, p, k)
                ahi[r : r + 64, lanes] = hi
                alo[r : r + 64, lanes] = (v - hi.astype(F32)).astype(BF16)

    mine = z * 2 + c
    panel_h = jnp.where(xh == xl, 0, 1)

    def block(first, scale, n):
        h = (n != ALL0).astype(jnp.int32)
        low, high = n != HIGH1, n != LOW1
        r0 = pl.multiple_of(first * 64, 64)

        def product(size):
            rows = pl.ds(pl.multiple_of(first // 2 * 128, 128), size)
            total = (
                jnp.dot(alo[rows, :], bhi[h], preferred_element_type=F32)
                + jnp.dot(ahi[rows, :], blo[h], preferred_element_type=F32)
                + jnp.dot(ahi[rows, :], bhi[h], preferred_element_type=F32)
            )
            for r in range(0, size, 64):
                keep = (scale > 0) | (first % 2 == r // 64)
                here = pl.ds(pl.multiple_of(first // 2 * 128 + r, 64), 64)

                @pl.when(low & keep)
                def _():
                    cbuf[h, here, :128] = total[r : r + 64, :128]

                @pl.when(high & keep)
                def _():
                    cbuf[h, here, 128:] = total[r : r + 64, 128:]

        pl.when(scale < 2)(lambda: product(128))
        pl.when(scale == 2)(lambda: product(256))
        pl.when(scale == 3)(lambda: product(384))

        @pl.when((panel_h == h) & ((low & (xl == 0)) | (high & (xl == 1))))
        def _():
            lanes = pl.ds(pl.multiple_of(xl * 128, 128), 128)

            @pl.loop(0, 2 * (1 + scale + scale // 2 + scale // 3))
            def _(i):
                bb, g = (2 * first + i) // 4, (2 * first + i) % 4
                s, both = (bb + 1) // 2, ((bb == 0) | (bb == 7)).astype(jnp.int32)
                k = both * (g // 2) + (1 - both) * ((bb + 1) % 2)
                up = (1 - both) * (g // 2)
                zz = (z + 8 + (2 * up - 1) * s) % 8
                x = 2 * (xh + k - 2 * xh * k) + g % 2
                v = abuf[zz, x, :, :, mine].reshape(32, 128)
                o = occ_col[k, pl.ds(pl.multiple_of(g % 2 * 256 + zz * 32, 32), 32), :]
                cbuf[h, pl.ds(pl.multiple_of(r0 + 32 * i, 32), 32), lanes] += v * (vsum[h, 0:1, lanes] - o)

    def c_copy(s, k, n):
        h, l0, nl = CHUNKS[n]
        q = 3 if h == 0 else 1 + k
        size, lanes = START[s + 1] - START[s], slice(l0, l0 + nl)
        src = cbuf.at[h, rows_at(s, 0, k) : rows_at(s, 0, k) + size, lanes]
        dst = rbuf.at[q - 1, START[s] : START[s] + size, lanes]
        return remote(src, dst, cr.at[s], xdev[q])

    def c_send(*what):
        go(lambda: c_copy(*what))

    def finish(s):
        arrive(rbuf.at[:, START[s] : START[s + 1]], cr.at[s])
        for p in sides(s):
            zz = zof(s, p)
            for l in range(2):
                r, t = rows_at(s, p, 0) + l * 32, START[s] + p * 64 + l * 32
                here, there = slice(r, r + 32), slice(t, t + 32)
                at = pl.ds(pl.multiple_of(l * 256 + zz * 32, 32), 32)
                total = (cbuf[0, here, :] + rbuf[2, there, :]) + (rbuf[0, there, :] + rbuf[1, there, :])
                o = occ_col[0, at, :]
                d = vsum[0, 0:1, :] - jnp.concatenate([o, o], axis=1)
                obuf[at, :] = (obuf[at, :] + total) / d
                pltpu.make_async_copy(obuf.at[at], out_ref.at[at], os).start()

    pl.semaphore_wait(barrier, 8)
    for d in range(2):
        z_send(0, 0, d)
    for q in (1, 2, 3):
        x_send(q)
    y_send(ALL0, 0)
    y_send(ALL0, 1)
    for copy in local:
        copy.wait()
    occ_row[0] = lookup(of_ref, oe_ref) + lookup(os_ref, oe_ref)
    vsum[0] = lookup(vf_ref, ve_ref) + lookup(vs_ref, ve_ref)
    go(lambda: remote(occ_row.at[0], occ_row.at[1], tr.at[0], xdev[3]))
    go(lambda: remote(vsum.at[0], vsum.at[1], tr.at[1], xdev[1]))
    e_send(LOW1)
    e_send(HIGH1)
    z_step(1, 0)
    x_step(2)
    y_wait(ALL0, 0)
    y_forward(ALL0)
    own_b.wait()
    split_b(ALL0, y)
    x_step(3)
    x_step(1)
    own_a.wait()
    sib_send(0, 0)
    z_step(1, 2)
    e_wait(LOW1)
    y_send(LOW1, 0)
    y_send(LOW1, 1)
    occ_col[0] = jnp.broadcast_to(occ_row[0, 0:1, :], (128, 512)).T
    arrive(occ_row.at[1], tr.at[0])
    arrive(vsum.at[1], tr.at[1])
    occ_col[1] = jnp.broadcast_to(occ_row[1, 0:1, :], (128, 512)).T
    y_wait(ALL0, 1)
    split_b(ALL0, ym)
    split_b(ALL0, yp)
    z_step(1, 3)
    sib_send(1, 1)
    sib_wait(0, 0)
    for k in range(2):
        split_a(0, k)
    split_b(LOW1, y)
    z_step(1, 1)
    sib_send(1, 0)
    sib_wait(1, 1)
    split_a(1, 1)
    y_far(ALL0)
    split_b(ALL0, y2)
    z_step(2, 2)

    before = [[] for _ in ORDER]

    def at(j, f, *a):
        before[j].append(lambda: f(*a))

    at(0, sib_wait, 1, 0)
    at(0, split_a, 1, 0)
    at(1, c_send, 0, 1, ALL0)
    at(1, c_send, 1, 1, ALL0)
    at(1, y_wait, LOW1, 0)
    at(1, y_forward, LOW1)
    at(1, e_wait, HIGH1)
    at(1, y_send, HIGH1, 0)
    at(1, y_send, HIGH1, 1)
    at(1, split_b, HIGH1, y)
    at(1, z_step, 2, 3)
    at(1, sib_send, 2, 1)
    at(1, sib_wait, 2, 1)
    at(1, split_a, 2, 1)
    at(2, c_send, 2, 1, ALL0)
    at(2, z_pair, 2, 0, 0)
    for q in (0, 1):
        at(2, z_send, 2, q, q)
    at(2, sib_send, 2, 0)
    at(2, y_wait, LOW1, 1)
    at(2, split_b, LOW1, ym)
    at(2, split_b, LOW1, yp)
    at(2, y_far, LOW1)
    at(2, split_b, LOW1, y2)
    at(3, c_send, 0, 0, LOW1)
    at(3, c_send, 0, 1, LOW1)
    at(3, c_send, 1, 0, LOW1)
    at(3, c_send, 1, 1, LOW1)
    at(3, z_step, 3, 2)
    at(3, sib_wait, 2, 0)
    at(3, split_a, 2, 0)
    at(4, c_send, 2, 0, LOW1)
    at(4, c_send, 2, 1, LOW1)
    at(4, y_wait, HIGH1, 0)
    at(4, y_forward, HIGH1)
    at(5, z_step, 3, 3)
    for q in (0, 1):
        at(5, z_send, 2, q, 1 - q)
    at(5, sib_send, 3, 1)
    at(5, sib_wait, 3, 1)
    at(5, split_a, 3, 1)
    at(6, c_send, 3, 1, ALL0)
    at(6, z_pair, 3, 0, 0)
    for q in (0, 1):
        at(6, z_send, 3, q, q)
    at(6, y_wait, HIGH1, 1)
    at(6, split_b, HIGH1, ym)
    at(6, split_b, HIGH1, yp)
    at(6, y_far, HIGH1)
    at(6, split_b, HIGH1, y2)
    at(7, c_send, 1, 0, HIGH1)
    at(7, c_send, 1, 1, HIGH1)
    at(7, c_send, 0, 0, HIGH1)
    at(7, c_send, 0, 1, HIGH1)
    at(7, z_pair, 4, 2, 0)
    for q in (2, 3):
        at(7, sib_quarter, q)
    at(8, c_send, 2, 0, HIGH1)
    at(8, c_send, 2, 1, HIGH1)
    at(8, z_pair, 3, 0, 1)
    at(8, sib_send, 3, 0)
    at(9, c_send, 3, 1, ALL1)
    at(9, sib_wait, 4, 1)
    at(9, split_a, 4, 1)
    at(10, c_send, 4, 1, ALL0)
    at(10, sib_wait, 3, 0)
    at(10, split_a, 3, 0)
    at(11, c_send, 3, 0, ALL1)
    at(11, z_pair, 4, 0, 0)
    for q in (0, 1):
        at(11, sib_quarter, q)
    at(12, c_send, 4, 1, ALL1)
    at(12, own_o.wait)
    at(12, sib_wait, 4, 0)
    at(12, split_a, 4, 0)
    at(13, c_send, 4, 0, ALL1)

    @pl.loop(0, len(ORDER))
    def _(j):
        def run(first, end):
            if end - first == 1:
                for step in before[first]:
                    step()
            else:
                middle = (first + end) // 2
                pl.when(j < middle)(lambda: run(first, middle))
                pl.when(j >= middle)(lambda: run(middle, end))

        run(0, len(ORDER))

        def pick(values):
            result = values[0]
            for i in range(1, len(values)):
                if values[i] != values[i - 1]:
                    result += (values[i] - values[i - 1]) * (j >= i).astype(jnp.int32)
            return result

        block(*(pick([o[i] for o in ORDER]) for i in range(3)))

    for s in range(5):
        finish(s)
    for make in sent:
        make().wait_send()
    pltpu.make_async_copy(obuf, out_ref, os).wait()


def local(amplitudes, integrals, other_terms, of, os_, vf, vs, oe, ve):
    a = amplitudes.reshape(2, 8, 64, 128).transpose(0, 2, 1, 3).reshape(2, 2, 16, 2, 8, 128)
    b = integrals.reshape(4, 2, 128, 256)
    small = [v.reshape(1, -1) for v in (of, os_, vf, vs, oe)] + [ve]
    hbm = pl.BlockSpec(memory_space=pltpu.HBM)
    dma = pltpu.SemaphoreType.DMA
    return pl.pallas_call(
        kernel,
        out_shape=jax.ShapeDtypeStruct((512, 256), F32),
        in_specs=[hbm] * 9,
        out_specs=pl.BlockSpec(memory_space=pl.ANY),
        scratch_shapes=[
            pltpu.VMEM((8, 4, 2, 2, 16, 8, 128), F32),
            pltpu.VMEM((1024, 2048), BF16),
            pltpu.VMEM((1024, 2048), BF16),
            pltpu.VMEM((2, 4, 4, 128, 256), F32),
            pltpu.VMEM((2, 2048, 256), BF16),
            pltpu.VMEM((2, 2048, 256), BF16),
            pltpu.VMEM((2, 1024, 256), F32),
            pltpu.VMEM((3, 512, 256), F32),
            pltpu.VMEM((2, 8, 512), F32),
            pltpu.VMEM((2, 512, 128), F32),
            pltpu.VMEM((2, 8, 256), F32),
            pltpu.VMEM((512, 256), F32),
            *[pltpu.VMEM(v.shape, v.dtype) for v in small],
            dma((9,)), dma((21,)), dma((3,)), dma((9,)), dma((9,)), dma((2,)), dma((5,)), dma((2,)), dma, dma,
        ],
        compiler_params=pltpu.CompilerParams(
            collective_id=0, has_side_effects=True, vmem_limit_bytes=213 << 18
        ),
        cost_estimate=pl.CostEstimate(flops=6442450944, bytes_accessed=4 << 20, transcendentals=0),
    )(a, b, other_terms, *small)


def solution(mesh):
    in_specs = (
        P(("col", "row"), None),
        P("col", "row"),
        P("col", "row"),
        P("col"),
        P("col"),
        P("row"),
        P("row"),
        P(),
        P(),
    )
    return jax.shard_map(local, mesh=mesh, in_specs=in_specs, out_specs=P("col", "row"), check_vma=False)
```

```python
import jax
import jax.numpy as jnp
from jax import lax
from jax.experimental import pallas as pl
from jax.experimental.pallas import tpu as pltpu
from jax.sharding import PartitionSpec as P

MESH = pl.DeviceIdType.MESH
F32, BF16 = jnp.float32, jnp.bfloat16
START = (0, 64, 192, 320, 448, 512)
CHUNKS = ((0, 0, 256), (1, 0, 128), (1, 128, 128), (1, 0, 256))
ALL0, LOW1, HIGH1, ALL1 = range(4)
ROWS = (64, 128, 256, 384)
ORDER = (
    (0, 3, ALL0), (8, 1, ALL0), (0, 3, LOW1), (6, 2, LOW1), (6, 1, ALL0), (12, 1, ALL0),
    (0, 3, HIGH1), (6, 2, HIGH1), (12, 1, ALL1), (15, 0, ALL0), (10, 1, ALL1), (15, 0, ALL1),
    (14, 0, ALL1), (10, 1, ALL0), (14, 0, ALL0),
)


def lookup(index_ref, table_ref):
    n = table_ref.shape[-1]
    onehot = (lax.broadcasted_iota(jnp.int32, (n, index_ref.shape[1]), 0) == index_ref[...]).astype(F32)
    table = jnp.broadcast_to(table_ref[...].reshape(1, n), (8, n))
    return jnp.dot(table, onehot, precision=lax.Precision.HIGHEST, preferred_element_type=F32)


def kernel(
    a_ref, b_ref, other_ref, *refs
):
    small, out_ref, refs = refs[:6], refs[6], refs[7:]
    abuf, ahi, alo, bbuf, bhi, blo, cbuf, rbuf, occ_row, occ_col, vsum, obuf = refs[:12]
    small_v, (loc, zr, xr, sr, yr, er, cr, tr, os, sends) = refs[12:18], refs[18:]
    of_ref, os_ref, vf_ref, vs_ref, oe_ref, ve_ref = small_v
    row, col = lax.axis_index("row"), lax.axis_index("col")
    xl, z, c = row // 16, (row // 2) % 8, row % 2
    xh, y = col // 4, col % 4

    def dev(xh, xl, y, z, c):
        return (xl * 16 + z * 2 + c, xh * 4 + y)

    px = ((xh, xl), (xh, 1 - xl), (1 - xh, 1 - xl), (1 - xh, xl))
    xi = [h * 2 + l for h, l in px]
    xdev = [dev(h, l, y, z, c) for h, l in px]
    zp, zm = (z + 1) % 8, (z + 7) % 8
    yp, ym, y2 = (y + 1) % 4, (y + 3) % 4, (y + 2) % 4
    zdev = (dev(xh, xl, y, zp, c), dev(xh, xl, y, zm, c))
    ydev = (dev(xh, xl, yp, z, c), dev(xh, xl, ym, z, c))
    sib = dev(xh, xl, y, z, 1 - c)

    def sides(s):
        return range(1 if s in (0, 4) else 2)

    zs_of = [((z + 8 - s) % 8, (z + s) % 8) for s in range(5)]

    def zof(s, p):
        return zs_of[s][p]

    def remote(src, dst, recv, to):
        return pltpu.make_async_remote_copy(
            src_ref=src, dst_ref=dst, send_sem=sends, recv_sem=recv, device_id=to, device_id_type=MESH
        )

    sent = []

    def go(make):
        make().start()
        sent.append(make)

    barrier = pltpu.get_barrier_semaphore()
    for to in (*xdev[1:], *zdev, *ydev, sib):
        pl.semaphore_signal(barrier, inc=1, device_id=to, device_id_type=MESH)
    local = [pltpu.make_async_copy(src, dst, loc.at[i]) for i, (src, dst) in enumerate(zip(small, small_v))]
    own_a = pltpu.make_async_copy(a_ref.at[:, xh, :, xl], abuf.at[z, xi[0], c], loc.at[6])
    own_b = pltpu.make_async_copy(b_ref.at[:, xl], bbuf.at[0, y], loc.at[7])
    own_o = pltpu.make_async_copy(other_ref, obuf, loc.at[8])
    for copy in (own_a, *local, own_b, own_o):
        copy.start()

    def arrive(at, recv):
        remote(at, at, recv, sib).wait_recv()

    def z_sem(s, q, d):
        if s == 1:
            return zr.at[2 * q + d]
        if s == 4:
            return zr.at[8 + q // 2]
        if q > 1:
            return zr.at[6 + 4 * (s - 2) + 2 * q + d]
        return zr.at[18 if s == 2 else 19 + (q + d) % 2]

    def z_send(s, q, d):
        def make():
            where = abuf.at[zof(s, d), xi[q], c]
            src = a_ref.at[:, xh, :, xl] if s == 0 and q == 0 else where
            return remote(src, where, z_sem(s + 1, q, d), zdev[d])

        go(make)

    def z_pair(s, q, d):
        at = abuf.at[zof(s, d), pl.ds(0, 2)] if s == 2 else abuf.at[zof(s, d), xi[q]]
        arrive(at, z_sem(s, q, d))

    def z_step(s, q):
        for d in (q % 2, 1 - q % 2):
            arrive(abuf.at[zof(s, d), xi[q], c], z_sem(s, q, d))
            if s < 3 or d == q % 2:
                z_send(s, q, d)

    def x_send(q):
        go(lambda: remote(a_ref.at[:, px[q][0], :, px[q][1]], abuf.at[z, xi[0], c], xr.at[q - 1], xdev[q]))

    def x_step(q):
        arrive(abuf.at[z, xi[q], c], xr.at[q - 1])
        for d in range(2):
            z_send(0, q, d)

    def sib_at(s, p, k, core):
        pair = pl.ds(2 * (xh if k == 0 else 1 - xh), 2)
        return abuf.at[zof(s, p), pair if s else slice(None), core]

    def sib_sem(s, k):
        return sr.at[0 if s == 0 else 2 * s - 1 + k]

    def sib_send(s, k):
        for p in sides(s):

            def make(p=p):
                where = sib_at(s, p, k, c)
                return remote(where, where, sib_sem(s, k), sib)

            go(make)

    def sib_quarter(q):
        def make():
            where = abuf.at[zof(4, 0), xi[q], c]
            return remote(where, where, sib_sem(4, q // 2), sib)

        go(make)

    def sib_wait(s, k):
        arrive(abuf.at[zof(s, 0), :, 1 - c] if s < 4 else sib_at(s, 0, k, 1 - c), sib_sem(s, k))

    def b_at(n, yy, groups=slice(None)):
        h, l0, nl = CHUNKS[n]
        return bbuf.at[h, yy, groups, :, l0 : l0 + nl]

    def part(i, d):
        return pl.ds(2 * (i if d == 0 else 1 - i), 2)

    def y_send(n, i):
        h, l0, nl = CHUNKS[n]
        for d in range(2):

            def make(d=d):
                src = b_ref.at[part(i, d), xl, :, l0 : l0 + nl] if h == 0 else b_at(n, y, part(i, d))
                return remote(src, b_at(n, y, part(i, d)), yr.at[n * 3 + i], ydev[d])

            go(make)

    def y_wait(n, i):
        arrive(b_at(n, ym), yr.at[n * 3 + i])

    def y_forward(n):
        for d in range(2):

            def make(d=d):
                at = b_at(n, (ym, yp)[d], part(0, d))
                return remote(at, at, yr.at[n * 3 + 2], ydev[d])

            go(make)

    def y_far(n):
        arrive(b_at(n, y2), yr.at[n * 3 + 2])

    def e_send(n):
        h, l0, nl = CHUNKS[n]
        go(lambda: remote(b_ref.at[:, 1 - xl, :, l0 : l0 + nl], b_at(n, y), er.at[n - LOW1], xdev[1]))

    def e_wait(n):
        arrive(b_at(n, y), er.at[n - LOW1])

    def split_b(n, yy):
        h, l0, nl = CHUNKS[n]
        lanes = slice(l0, l0 + nl)

        @pl.loop(0, 16)
        def _(i):
            g, r = i // 4, pl.multiple_of((i % 4) * 32, 32)
            v = bbuf[h, yy, g, pl.ds(r, 32), lanes]
            hi = v.astype(BF16)
            to = pl.ds(pl.multiple_of(yy * 512 + g * 128 + r, 32), 32)
            bhi[h, to, lanes] = hi
            blo[h, to, lanes] = (v - hi.astype(F32)).astype(BF16)

    def rows_at(s, p, k):
        return (64 * k if s in (0, 4) else 128 * k - 128) + 256 * s - (128 if s == 4 else 0) + 64 * p

    def split_a(s, k):
        @pl.loop(0, 16)
        def _(j):
            lanes = pl.ds(pl.multiple_of(j * 128, 128), 128)
            for p in sides(s):
                v = abuf[zof(s, p), pl.ds(2 * (xh if k == 0 else 1 - xh), 2), :, :, j].reshape(64, 128)
                hi = v.astype(BF16)
                r = rows_at(s, p, k)
                ahi[r : r + 64, lanes] = hi
                alo[r : r + 64, lanes] = (v - hi.astype(F32)).astype(BF16)

    mine = z * 2 + c
    panel_h = jnp.where(xh == xl, 0, 1)

    def block(first, scale, n):
        h = (n != ALL0).astype(jnp.int32)
        low, high = n != HIGH1, n != LOW1
        r0 = pl.multiple_of(first * 64, 64)

        def product(size):
            rows = pl.ds(pl.multiple_of(first // 2 * 128, 128), size)
            total = (
                jnp.dot(alo[rows, :], bhi[h], preferred_element_type=F32)
                + jnp.dot(ahi[rows, :], blo[h], preferred_element_type=F32)
                + jnp.dot(ahi[rows, :], bhi[h], preferred_element_type=F32)
            )
            for r in range(0, size, 64):
                keep = (scale > 0) | (first % 2 == r // 64)
                here = pl.ds(pl.multiple_of(first // 2 * 128 + r, 64), 64)

                @pl.when(low & keep)
                def _():
                    cbuf[h, here, :128] = total[r : r + 64, :128]

                @pl.when(high & keep)
                def _():
                    cbuf[h, here, 128:] = total[r : r + 64, 128:]

        pl.when(scale < 2)(lambda: product(128))
        pl.when(scale == 2)(lambda: product(256))
        pl.when(scale == 3)(lambda: product(384))

        @pl.when((panel_h == h) & ((low & (xl == 0)) | (high & (xl == 1))))
        def _():
            lanes = pl.ds(pl.multiple_of(xl * 128, 128), 128)

            @pl.loop(0, 2 * (1 + scale + scale // 2 + scale // 3))
            def _(i):
                bb, g = (2 * first + i) // 4, (2 * first + i) % 4
                s, both = (bb + 1) // 2, ((bb == 0) | (bb == 7)).astype(jnp.int32)
                k = both * (g // 2) + (1 - both) * ((bb + 1) % 2)
                up = (1 - both) * (g // 2)
                zz = (z + 8 + (2 * up - 1) * s) % 8
                x = 2 * (xh + k - 2 * xh * k) + g % 2
                v = abuf[zz, x, :, :, mine].reshape(32, 128)
                o = occ_col[k, pl.ds(pl.multiple_of(g % 2 * 256 + zz * 32, 32), 32), :]
                cbuf[h, pl.ds(pl.multiple_of(r0 + 32 * i, 32), 32), lanes] += v * (vsum[h, 0:1, lanes] - o)

    def c_copy(s, k, n):
        h, l0, nl = CHUNKS[n]
        q = 3 if h == 0 else 1 + k
        size, lanes = START[s + 1] - START[s], slice(l0, l0 + nl)
        src = cbuf.at[h, rows_at(s, 0, k) : rows_at(s, 0, k) + size, lanes]
        dst = rbuf.at[q - 1, START[s] : START[s] + size, lanes]
        return remote(src, dst, cr.at[s], xdev[q])

    def c_send(*what):
        go(lambda: c_copy(*what))

    def finish(s):
        arrive(rbuf.at[:, START[s] : START[s + 1]], cr.at[s])
        for p in sides(s):
            zz = zof(s, p)
            for l in range(2):
                r, t = rows_at(s, p, 0) + l * 32, START[s] + p * 64 + l * 32
                here, there = slice(r, r + 32), slice(t, t + 32)
                at = pl.ds(pl.multiple_of(l * 256 + zz * 32, 32), 32)
                total = (cbuf[0, here, :] + rbuf[2, there, :]) + (rbuf[0, there, :] + rbuf[1, there, :])
                o = occ_col[0, at, :]
                d = vsum[0, 0:1, :] - jnp.concatenate([o, o], axis=1)
                obuf[at, :] = (obuf[at, :] + total) / d
                pltpu.make_async_copy(obuf.at[at], out_ref.at[at], os).start()

    pl.semaphore_wait(barrier, 8)
    for d in range(2):
        z_send(0, 0, d)
    for q in (1, 2, 3):
        x_send(q)
    y_send(ALL0, 0)
    y_send(ALL0, 1)
    for copy in local:
        copy.wait()
    occ_row[0] = lookup(of_ref, oe_ref) + lookup(os_ref, oe_ref)
    vsum[0] = lookup(vf_ref, ve_ref) + lookup(vs_ref, ve_ref)
    go(lambda: remote(occ_row.at[0], occ_row.at[1], tr.at[0], xdev[3]))
    go(lambda: remote(vsum.at[0], vsum.at[1], tr.at[1], xdev[1]))
    e_send(LOW1)
    e_send(HIGH1)
    z_step(1, 0)
    x_step(2)
    y_wait(ALL0, 0)
    y_forward(ALL0)
    own_b.wait()
    split_b(ALL0, y)
    x_step(3)
    x_step(1)
    own_a.wait()
    sib_send(0, 0)
    z_step(1, 2)
    e_wait(LOW1)
    y_send(LOW1, 0)
    y_send(LOW1, 1)
    occ_col[0] = jnp.broadcast_to(occ_row[0, 0:1, :], (128, 512)).T
    arrive(occ_row.at[1], tr.at[0])
    arrive(vsum.at[1], tr.at[1])
    occ_col[1] = jnp.broadcast_to(occ_row[1, 0:1, :], (128, 512)).T
    y_wait(ALL0, 1)
    split_b(ALL0, ym)
    split_b(ALL0, yp)
    z_step(1, 3)
    sib_send(1, 1)
    sib_wait(0, 0)
    for k in range(2):
        split_a(0, k)
    split_b(LOW1, y)
    z_step(1, 1)
    sib_send(1, 0)
    sib_wait(1, 1)
    split_a(1, 1)
    y_far(ALL0)
    split_b(ALL0, y2)
    z_step(2, 2)

    before = [[] for _ in ORDER]

    def at(j, f, *a):
        before[j].append(lambda: f(*a))

    at(0, sib_wait, 1, 0)
    at(0, split_a, 1, 0)
    at(1, c_send, 0, 1, ALL0)
    at(1, c_send, 1, 1, ALL0)
    at(1, y_wait, LOW1, 0)
    at(1, y_forward, LOW1)
    at(1, e_wait, HIGH1)
    at(1, y_send, HIGH1, 0)
    at(1, y_send, HIGH1, 1)
    at(1, split_b, HIGH1, y)
    at(1, z_step, 2, 3)
    at(1, sib_send, 2, 1)
    at(1, sib_wait, 2, 1)
    at(1, split_a, 2, 1)
    at(2, c_send, 2, 1, ALL0)
    at(2, z_pair, 2, 0, 0)
    for q in (0, 1):
        at(2, z_send, 2, q, q)
    at(2, sib_send, 2, 0)
    at(2, y_wait, LOW1, 1)
    at(2, split_b, LOW1, ym)
    at(2, split_b, LOW1, yp)
    at(2, y_far, LOW1)
    at(2, split_b, LOW1, y2)
    at(3, c_send, 0, 0, LOW1)
    at(3, c_send, 0, 1, LOW1)
    at(3, c_send, 1, 0, LOW1)
    at(3, c_send, 1, 1, LOW1)
    at(3, z_step, 3, 2)
    at(3, sib_wait, 2, 0)
    at(3, split_a, 2, 0)
    at(4, c_send, 2, 0, LOW1)
    at(4, c_send, 2, 1, LOW1)
    at(4, y_wait, HIGH1, 0)
    at(4, y_forward, HIGH1)
    at(4, z_step, 3, 3)
    for q in (0, 1):
        at(4, z_send, 2, q, 1 - q)
    at(4, sib_send, 3, 1)
    at(5, sib_wait, 3, 1)
    at(5, split_a, 3, 1)
    at(6, c_send, 3, 1, ALL0)
    at(6, z_pair, 3, 0, 0)
    for q in (0, 1):
        at(6, z_send, 3, q, q)
    at(6, y_wait, HIGH1, 1)
    at(6, split_b, HIGH1, ym)
    at(6, split_b, HIGH1, yp)
    at(6, y_far, HIGH1)
    at(6, split_b, HIGH1, y2)
    at(7, c_send, 1, 0, HIGH1)
    at(7, c_send, 1, 1, HIGH1)
    at(7, c_send, 0, 0, HIGH1)
    at(7, c_send, 0, 1, HIGH1)
    at(7, z_pair, 4, 2, 0)
    for q in (2, 3):
        at(7, sib_quarter, q)
    at(8, c_send, 2, 0, HIGH1)
    at(8, c_send, 2, 1, HIGH1)
    at(8, z_pair, 3, 0, 1)
    at(8, sib_send, 3, 0)
    at(9, c_send, 3, 1, ALL1)
    at(9, sib_wait, 4, 1)
    at(9, split_a, 4, 1)
    at(10, c_send, 4, 1, ALL0)
    at(10, sib_wait, 3, 0)
    at(10, split_a, 3, 0)
    at(11, c_send, 3, 0, ALL1)
    at(11, z_pair, 4, 0, 0)
    for q in (0, 1):
        at(11, sib_quarter, q)
    at(12, c_send, 4, 1, ALL1)
    at(12, own_o.wait)
    at(12, sib_wait, 4, 0)
    at(12, split_a, 4, 0)
    at(13, c_send, 4, 0, ALL1)

    @pl.loop(0, len(ORDER))
    def _(j):
        def run(first, end):
            if end - first == 1:
                for step in before[first]:
                    step()
            else:
                middle = (first + end) // 2
                pl.when(j < middle)(lambda: run(first, middle))
                pl.when(j >= middle)(lambda: run(middle, end))

        run(0, len(ORDER))

        def pick(values):
            result = values[0]
            for i in range(1, len(values)):
                if values[i] != values[i - 1]:
                    result += (values[i] - values[i - 1]) * (j >= i).astype(jnp.int32)
            return result

        block(*(pick([o[i] for o in ORDER]) for i in range(3)))

    for s in range(5):
        finish(s)
    for make in sent:
        make().wait_send()
    pltpu.make_async_copy(obuf, out_ref, os).wait()


def local(amplitudes, integrals, other_terms, of, os_, vf, vs, oe, ve):
    a = amplitudes.reshape(2, 8, 64, 128).transpose(0, 2, 1, 3).reshape(2, 2, 16, 2, 8, 128)
    b = integrals.reshape(4, 2, 128, 256)
    small = [v.reshape(1, -1) for v in (of, os_, vf, vs, oe)] + [ve]
    hbm = pl.BlockSpec(memory_space=pltpu.HBM)
    dma = pltpu.SemaphoreType.DMA
    return pl.pallas_call(
        kernel,
        out_shape=jax.ShapeDtypeStruct((512, 256), F32),
        in_specs=[hbm] * 9,
        out_specs=pl.BlockSpec(memory_space=pl.ANY),
        scratch_shapes=[
            pltpu.VMEM((8, 4, 2, 2, 16, 8, 128), F32),
            pltpu.VMEM((1024, 2048), BF16),
            pltpu.VMEM((1024, 2048), BF16),
            pltpu.VMEM((2, 4, 4, 128, 256), F32),
            pltpu.VMEM((2, 2048, 256), BF16),
            pltpu.VMEM((2, 2048, 256), BF16),
            pltpu.VMEM((2, 1024, 256), F32),
            pltpu.VMEM((3, 512, 256), F32),
            pltpu.VMEM((2, 8, 512), F32),
            pltpu.VMEM((2, 512, 128), F32),
            pltpu.VMEM((2, 8, 256), F32),
            pltpu.VMEM((512, 256), F32),
            *[pltpu.VMEM(v.shape, v.dtype) for v in small],
            dma((9,)), dma((21,)), dma((3,)), dma((9,)), dma((9,)), dma((2,)), dma((5,)), dma((2,)), dma, dma,
        ],
        compiler_params=pltpu.CompilerParams(
            collective_id=0, has_side_effects=True, vmem_limit_bytes=213 << 18
        ),
        cost_estimate=pl.CostEstimate(flops=6442450944, bytes_accessed=4 << 20, transcendentals=0),
    )(a, b, other_terms, *small)


def solution(mesh):
    in_specs = (
        P(("col", "row"), None),
        P("col", "row"),
        P("col", "row"),
        P("col"),
        P("col"),
        P("row"),
        P("row"),
        P(),
        P(),
    )
    return jax.shard_map(local, mesh=mesh, in_specs=in_specs, out_specs=P("col", "row"), check_vma=False)
```

```python
import jax
import jax.numpy as jnp
from jax import lax
from jax.experimental import pallas as pl
from jax.experimental.pallas import tpu as pltpu
from jax.sharding import PartitionSpec as P

MESH = pl.DeviceIdType.MESH
F32, BF16 = jnp.float32, jnp.bfloat16
START = (0, 64, 192, 320, 448, 512)
CHUNKS = ((0, 0, 256), (1, 0, 128), (1, 128, 128), (1, 0, 256))
ALL0, LOW1, HIGH1, ALL1 = range(4)
ROWS = (64, 128, 256, 384)
ORDER = (
    (0, 3, ALL0), (8, 1, ALL0), (0, 3, LOW1), (6, 2, LOW1), (6, 1, ALL0), (12, 1, ALL0),
    (0, 3, HIGH1), (6, 2, HIGH1), (12, 1, ALL1), (15, 0, ALL0), (10, 1, ALL1), (15, 0, ALL1),
    (14, 0, ALL1), (10, 1, ALL0), (14, 0, ALL0),
)


def lookup(index_ref, table_ref):
    n = table_ref.shape[-1]
    onehot = (lax.broadcasted_iota(jnp.int32, (n, index_ref.shape[1]), 0) == index_ref[...]).astype(F32)
    table = jnp.broadcast_to(table_ref[...].reshape(1, n), (8, n))
    return jnp.dot(table, onehot, precision=lax.Precision.HIGHEST, preferred_element_type=F32)


def kernel(
    a_ref, b_ref, other_ref, *refs
):
    small, out_ref, refs = refs[:6], refs[6], refs[7:]
    abuf, ahi, alo, bbuf, bhi, blo, cbuf, rbuf, occ_row, occ_col, vsum, obuf = refs[:12]
    small_v, (loc, zr, xr, sr, yr, er, cr, tr, os, sends) = refs[12:18], refs[18:]
    of_ref, os_ref, vf_ref, vs_ref, oe_ref, ve_ref = small_v
    row, col = lax.axis_index("row"), lax.axis_index("col")
    xl, z, c = row // 16, (row // 2) % 8, row % 2
    xh, y = col // 4, col % 4

    def dev(xh, xl, y, z, c):
        return (xl * 16 + z * 2 + c, xh * 4 + y)

    px = ((xh, xl), (xh, 1 - xl), (1 - xh, 1 - xl), (1 - xh, xl))
    xi = [h * 2 + l for h, l in px]
    xdev = [dev(h, l, y, z, c) for h, l in px]
    zp, zm = (z + 1) % 8, (z + 7) % 8
    yp, ym, y2 = (y + 1) % 4, (y + 3) % 4, (y + 2) % 4
    zdev = (dev(xh, xl, y, zp, c), dev(xh, xl, y, zm, c))
    ydev = (dev(xh, xl, yp, z, c), dev(xh, xl, ym, z, c))
    sib = dev(xh, xl, y, z, 1 - c)

    def sides(s):
        return range(1 if s in (0, 4) else 2)

    zs_of = [((z + 8 - s) % 8, (z + s) % 8) for s in range(5)]

    def zof(s, p):
        return zs_of[s][p]

    def remote(src, dst, recv, to):
        return pltpu.make_async_remote_copy(
            src_ref=src, dst_ref=dst, send_sem=sends, recv_sem=recv, device_id=to, device_id_type=MESH
        )

    sent = []

    def go(make):
        make().start()
        sent.append(make)

    barrier = pltpu.get_barrier_semaphore()
    for to in (*xdev[1:], *zdev, *ydev, sib):
        pl.semaphore_signal(barrier, inc=1, device_id=to, device_id_type=MESH)
    local = [pltpu.make_async_copy(src, dst, loc.at[i]) for i, (src, dst) in enumerate(zip(small, small_v))]
    own_a = pltpu.make_async_copy(a_ref.at[:, xh, :, xl], abuf.at[z, xi[0], c], loc.at[6])
    own_b = pltpu.make_async_copy(b_ref.at[:, xl], bbuf.at[0, y], loc.at[7])
    own_o = pltpu.make_async_copy(other_ref, obuf, loc.at[8])
    for copy in (own_a, *local, own_b, own_o):
        copy.start()

    def arrive(at, recv):
        remote(at, at, recv, sib).wait_recv()

    def z_sem(s, q, d):
        if s == 1:
            return zr.at[2 * q + d]
        if s == 4:
            return zr.at[8 + q // 2]
        if q > 1:
            return zr.at[6 + 4 * (s - 2) + 2 * q + d]
        return zr.at[18 if s == 2 else 19 + (q + d) % 2]

    def z_send(s, q, d):
        def make():
            where = abuf.at[zof(s, d), xi[q], c]
            src = a_ref.at[:, xh, :, xl] if s == 0 and q == 0 else where
            return remote(src, where, z_sem(s + 1, q, d), zdev[d])

        go(make)

    def z_pair(s, q, d):
        at = abuf.at[zof(s, d), pl.ds(0, 2)] if s == 2 else abuf.at[zof(s, d), xi[q]]
        arrive(at, z_sem(s, q, d))

    def z_step(s, q):
        for d in (q % 2, 1 - q % 2):
            arrive(abuf.at[zof(s, d), xi[q], c], z_sem(s, q, d))
            if s < 3 or d == q % 2:
                z_send(s, q, d)

    def x_send(q):
        go(lambda: remote(a_ref.at[:, px[q][0], :, px[q][1]], abuf.at[z, xi[0], c], xr.at[q - 1], xdev[q]))

    def x_step(q):
        arrive(abuf.at[z, xi[q], c], xr.at[q - 1])
        for d in range(2):
            z_send(0, q, d)

    def sib_at(s, p, k, core):
        pair = pl.ds(2 * (xh if k == 0 else 1 - xh), 2)
        return abuf.at[zof(s, p), pair if s else slice(None), core]

    def sib_sem(s, k):
        return sr.at[0 if s == 0 else 2 * s - 1 + k]

    def sib_send(s, k):
        for p in sides(s):

            def make(p=p):
                where = sib_at(s, p, k, c)
                return remote(where, where, sib_sem(s, k), sib)

            go(make)

    def sib_quarter(q):
        def make():
            where = abuf.at[zof(4, 0), xi[q], c]
            return remote(where, where, sib_sem(4, q // 2), sib)

        go(make)

    def sib_wait(s, k):
        arrive(abuf.at[zof(s, 0), :, 1 - c] if s < 4 else sib_at(s, 0, k, 1 - c), sib_sem(s, k))

    def b_at(n, yy, groups=slice(None)):
        h, l0, nl = CHUNKS[n]
        return bbuf.at[h, yy, groups, :, l0 : l0 + nl]

    def part(i, d):
        return pl.ds(2 * (i if d == 0 else 1 - i), 2)

    def y_send(n, i):
        h, l0, nl = CHUNKS[n]
        for d in range(2):

            def make(d=d):
                src = b_ref.at[part(i, d), xl, :, l0 : l0 + nl] if h == 0 else b_at(n, y, part(i, d))
                return remote(src, b_at(n, y, part(i, d)), yr.at[n * 3 + i], ydev[d])

            go(make)

    def y_wait(n, i):
        arrive(b_at(n, ym), yr.at[n * 3 + i])

    def y_forward(n):
        for d in range(2):

            def make(d=d):
                at = b_at(n, (ym, yp)[d], part(0, d))
                return remote(at, at, yr.at[n * 3 + 2], ydev[d])

            go(make)

    def y_far(n):
        arrive(b_at(n, y2), yr.at[n * 3 + 2])

    def e_send(n):
        h, l0, nl = CHUNKS[n]
        go(lambda: remote(b_ref.at[:, 1 - xl, :, l0 : l0 + nl], b_at(n, y), er.at[n - LOW1], xdev[1]))

    def e_wait(n):
        arrive(b_at(n, y), er.at[n - LOW1])

    def split_b(n, yy):
        h, l0, nl = CHUNKS[n]
        lanes = slice(l0, l0 + nl)

        @pl.loop(0, 16, unroll=2)
        def _(i):
            g, r = i // 4, pl.multiple_of((i % 4) * 32, 32)
            v = bbuf[h, yy, g, pl.ds(r, 32), lanes]
            hi = v.astype(BF16)
            to = pl.ds(pl.multiple_of(yy * 512 + g * 128 + r, 32), 32)
            bhi[h, to, lanes] = hi
            blo[h, to, lanes] = (v - hi.astype(F32)).astype(BF16)

    def rows_at(s, p, k):
        return (64 * k if s in (0, 4) else 128 * k - 128) + 256 * s - (128 if s == 4 else 0) + 64 * p

    def split_a(s, k):
        @pl.loop(0, 16, unroll=2)
        def _(j):
            lanes = pl.ds(pl.multiple_of(j * 128, 128), 128)
            for p in sides(s):
                v = abuf[zof(s, p), pl.ds(2 * (xh if k == 0 else 1 - xh), 2), :, :, j].reshape(64, 128)
                hi = v.astype(BF16)
                r = rows_at(s, p, k)
                ahi[r : r + 64, lanes] = hi
                alo[r : r + 64, lanes] = (v - hi.astype(F32)).astype(BF16)

    mine = z * 2 + c
    panel_h = jnp.where(xh == xl, 0, 1)

    def block(first, scale, n):
        h = (n != ALL0).astype(jnp.int32)
        low, high = n != HIGH1, n != LOW1
        r0 = pl.multiple_of(first * 64, 64)

        def product(size):
            rows = pl.ds(pl.multiple_of(first // 2 * 128, 128), size)
            total = (
                jnp.dot(alo[rows, :], bhi[h], preferred_element_type=F32)
                + jnp.dot(ahi[rows, :], blo[h], preferred_element_type=F32)
                + jnp.dot(ahi[rows, :], bhi[h], preferred_element_type=F32)
            )
            for r in range(0, size, 64):
                keep = (scale > 0) | (first % 2 == r // 64)
                here = pl.ds(pl.multiple_of(first // 2 * 128 + r, 64), 64)

                @pl.when(low & keep)
                def _():
                    cbuf[h, here, :128] = total[r : r + 64, :128]

                @pl.when(high & keep)
                def _():
                    cbuf[h, here, 128:] = total[r : r + 64, 128:]

        pl.when(scale < 2)(lambda: product(128))
        pl.when(scale == 2)(lambda: product(256))
        pl.when(scale == 3)(lambda: product(384))

        @pl.when((panel_h == h) & ((low & (xl == 0)) | (high & (xl == 1))))
        def _():
            lanes = pl.ds(pl.multiple_of(xl * 128, 128), 128)

            @pl.loop(0, 2 * (1 + scale + scale // 2 + scale // 3))
            def _(i):
                bb, g = (2 * first + i) // 4, (2 * first + i) % 4
                s, both = (bb + 1) // 2, ((bb == 0) | (bb == 7)).astype(jnp.int32)
                k = both * (g // 2) + (1 - both) * ((bb + 1) % 2)
                up = (1 - both) * (g // 2)
                zz = (z + 8 + (2 * up - 1) * s) % 8
                x = 2 * (xh + k - 2 * xh * k) + g % 2
                v = abuf[zz, x, :, :, mine].reshape(32, 128)
                o = occ_col[k, pl.ds(pl.multiple_of(g % 2 * 256 + zz * 32, 32), 32), :]
                cbuf[h, pl.ds(pl.multiple_of(r0 + 32 * i, 32), 32), lanes] += v * (vsum[h, 0:1, lanes] - o)

    def c_copy(s, k, n):
        h, l0, nl = CHUNKS[n]
        q = 3 if h == 0 else 1 + k
        size, lanes = START[s + 1] - START[s], slice(l0, l0 + nl)
        src = cbuf.at[h, rows_at(s, 0, k) : rows_at(s, 0, k) + size, lanes]
        dst = rbuf.at[q - 1, START[s] : START[s] + size, lanes]
        return remote(src, dst, cr.at[s], xdev[q])

    def c_send(*what):
        go(lambda: c_copy(*what))

    def finish(s):
        arrive(rbuf.at[:, START[s] : START[s + 1]], cr.at[s])
        for p in sides(s):
            zz = zof(s, p)
            for l in range(2):
                r, t = rows_at(s, p, 0) + l * 32, START[s] + p * 64 + l * 32
                here, there = slice(r, r + 32), slice(t, t + 32)
                at = pl.ds(pl.multiple_of(l * 256 + zz * 32, 32), 32)
                total = (cbuf[0, here, :] + rbuf[2, there, :]) + (rbuf[0, there, :] + rbuf[1, there, :])
                o = occ_col[0, at, :]
                d = vsum[0, 0:1, :] - jnp.concatenate([o, o], axis=1)
                obuf[at, :] = (obuf[at, :] + total) / d
                pltpu.make_async_copy(obuf.at[at], out_ref.at[at], os).start()

    pl.semaphore_wait(barrier, 8)
    for d in range(2):
        z_send(0, 0, d)
    for q in (1, 2, 3):
        x_send(q)
    y_send(ALL0, 0)
    y_send(ALL0, 1)
    for copy in local:
        copy.wait()
    occ_row[0] = lookup(of_ref, oe_ref) + lookup(os_ref, oe_ref)
    vsum[0] = lookup(vf_ref, ve_ref) + lookup(vs_ref, ve_ref)
    go(lambda: remote(occ_row.at[0], occ_row.at[1], tr.at[0], xdev[3]))
    go(lambda: remote(vsum.at[0], vsum.at[1], tr.at[1], xdev[1]))
    e_send(LOW1)
    e_send(HIGH1)
    z_step(1, 0)
    x_step(2)
    y_wait(ALL0, 0)
    y_forward(ALL0)
    own_b.wait()
    split_b(ALL0, y)
    x_step(3)
    x_step(1)
    own_a.wait()
    sib_send(0, 0)
    z_step(1, 2)
    e_wait(LOW1)
    y_send(LOW1, 0)
    y_send(LOW1, 1)
    occ_col[0] = jnp.broadcast_to(occ_row[0, 0:1, :], (128, 512)).T
    arrive(occ_row.at[1], tr.at[0])
    arrive(vsum.at[1], tr.at[1])
    occ_col[1] = jnp.broadcast_to(occ_row[1, 0:1, :], (128, 512)).T
    y_wait(ALL0, 1)
    split_b(ALL0, ym)
    split_b(ALL0, yp)
    z_step(1, 3)
    sib_send(1, 1)
    sib_wait(0, 0)
    for k in range(2):
        split_a(0, k)
    split_b(LOW1, y)
    z_step(1, 1)
    sib_send(1, 0)
    sib_wait(1, 1)
    split_a(1, 1)
    y_far(ALL0)
    split_b(ALL0, y2)
    z_step(2, 2)

    before = [[] for _ in ORDER]

    def at(j, f, *a):
        before[j].append(lambda: f(*a))

    at(0, sib_wait, 1, 0)
    at(0, split_a, 1, 0)
    at(0, y_wait, LOW1, 0)
    at(0, y_forward, LOW1)
    at(0, e_wait, HIGH1)
    at(0, y_send, HIGH1, 0)
    at(0, y_send, HIGH1, 1)
    at(1, c_send, 0, 1, ALL0)
    at(1, c_send, 1, 1, ALL0)
    at(1, split_b, HIGH1, y)
    at(1, z_step, 2, 3)
    at(1, sib_send, 2, 1)
    at(1, sib_wait, 2, 1)
    at(1, split_a, 2, 1)
    at(2, c_send, 2, 1, ALL0)
    at(2, y_wait, LOW1, 1)
    at(2, split_b, LOW1, ym)
    at(2, split_b, LOW1, yp)
    at(2, z_pair, 2, 0, 0)
    for q in (0, 1):
        at(2, z_send, 2, q, q)
    at(2, sib_send, 2, 0)
    at(2, y_far, LOW1)
    at(2, split_b, LOW1, y2)
    at(3, c_send, 0, 0, LOW1)
    at(3, c_send, 0, 1, LOW1)
    at(3, c_send, 1, 0, LOW1)
    at(3, c_send, 1, 1, LOW1)
    at(3, z_step, 3, 2)
    at(3, sib_wait, 2, 0)
    at(3, split_a, 2, 0)
    at(4, c_send, 2, 0, LOW1)
    at(4, c_send, 2, 1, LOW1)
    at(4, y_wait, HIGH1, 0)
    at(4, y_forward, HIGH1)
    at(4, z_step, 3, 3)
    for q in (0, 1):
        at(4, z_send, 2, q, 1 - q)
    at(4, sib_send, 3, 1)
    at(5, sib_wait, 3, 1)
    at(5, split_a, 3, 1)
    at(6, c_send, 3, 1, ALL0)
    at(6, z_pair, 3, 0, 0)
    for q in (0, 1):
        at(6, z_send, 3, q, q)
    at(6, y_wait, HIGH1, 1)
    at(6, split_b, HIGH1, ym)
    at(6, split_b, HIGH1, yp)
    at(6, y_far, HIGH1)
    at(6, split_b, HIGH1, y2)
    at(7, c_send, 1, 0, HIGH1)
    at(7, c_send, 1, 1, HIGH1)
    at(7, c_send, 0, 0, HIGH1)
    at(7, c_send, 0, 1, HIGH1)
    at(7, z_pair, 4, 2, 0)
    for q in (2, 3):
        at(7, sib_quarter, q)
    at(8, c_send, 2, 0, HIGH1)
    at(8, c_send, 2, 1, HIGH1)
    at(8, z_pair, 3, 0, 1)
    at(8, sib_send, 3, 0)
    at(9, c_send, 3, 1, ALL1)
    at(9, sib_wait, 4, 1)
    at(9, split_a, 4, 1)
    at(10, c_send, 4, 1, ALL0)
    at(10, sib_wait, 3, 0)
    at(10, split_a, 3, 0)
    at(10, z_pair, 4, 0, 0)
    for q in (0, 1):
        at(10, sib_quarter, q)
    at(11, c_send, 3, 0, ALL1)
    at(12, c_send, 4, 1, ALL1)
    at(12, own_o.wait)
    at(12, sib_wait, 4, 0)
    at(12, split_a, 4, 0)
    at(13, c_send, 4, 0, ALL1)

    @pl.loop(0, len(ORDER))
    def _(j):
        def run(first, end):
            if end - first == 1:
                for step in before[first]:
                    step()
            else:
                middle = (first + end) // 2
                pl.when(j < middle)(lambda: run(first, middle))
                pl.when(j >= middle)(lambda: run(middle, end))

        run(0, len(ORDER))

        def pick(values):
            result = values[0]
            for i in range(1, len(values)):
                if values[i] != values[i - 1]:
                    result += (values[i] - values[i - 1]) * (j >= i).astype(jnp.int32)
            return result

        block(*(pick([o[i] for o in ORDER]) for i in range(3)))

    for s in range(5):
        finish(s)
    for make in sent:
        make().wait_send()
    pltpu.make_async_copy(obuf, out_ref, os).wait()


def local(amplitudes, integrals, other_terms, of, os_, vf, vs, oe, ve):
    a = amplitudes.reshape(2, 8, 64, 128).transpose(0, 2, 1, 3).reshape(2, 2, 16, 2, 8, 128)
    b = integrals.reshape(4, 2, 128, 256)
    small = [v.reshape(1, -1) for v in (of, os_, vf, vs, oe)] + [ve]
    hbm = pl.BlockSpec(memory_space=pltpu.HBM)
    dma = pltpu.SemaphoreType.DMA
    return pl.pallas_call(
        kernel,
        out_shape=jax.ShapeDtypeStruct((512, 256), F32),
        in_specs=[hbm] * 9,
        out_specs=pl.BlockSpec(memory_space=pl.ANY),
        scratch_shapes=[
            pltpu.VMEM((8, 4, 2, 2, 16, 8, 128), F32),
            pltpu.VMEM((1024, 2048), BF16),
            pltpu.VMEM((1024, 2048), BF16),
            pltpu.VMEM((2, 4, 4, 128, 256), F32),
            pltpu.VMEM((2, 2048, 256), BF16),
            pltpu.VMEM((2, 2048, 256), BF16),
            pltpu.VMEM((2, 1024, 256), F32),
            pltpu.VMEM((3, 512, 256), F32),
            pltpu.VMEM((2, 8, 512), F32),
            pltpu.VMEM((2, 512, 128), F32),
            pltpu.VMEM((2, 8, 256), F32),
            pltpu.VMEM((512, 256), F32),
            *[pltpu.VMEM(v.shape, v.dtype) for v in small],
            dma((9,)), dma((21,)), dma((3,)), dma((9,)), dma((9,)), dma((2,)), dma((5,)), dma((2,)), dma, dma,
        ],
        compiler_params=pltpu.CompilerParams(
            collective_id=0, has_side_effects=True, vmem_limit_bytes=213 << 18
        ),
        cost_estimate=pl.CostEstimate(flops=6442450944, bytes_accessed=4 << 20, transcendentals=0),
    )(a, b, other_terms, *small)


def solution(mesh):
    in_specs = (
        P(("col", "row"), None),
        P("col", "row"),
        P("col", "row"),
        P("col"),
        P("col"),
        P("row"),
        P("row"),
        P(),
        P(),
    )
    return jax.shard_map(local, mesh=mesh, in_specs=in_specs, out_specs=P("col", "row"), check_vma=False)
```
